256 devices in a mesh: seq: 128 (over x, z, y_hi, core), head: 2 (over y_lo).
Axes of the slice: x: 4, y: 4 (y_hi: 2, y_lo: 2; y = y_hi * 2 + y_lo), z: 8, core: 2. Of those that a mesh axis runs over, the one named last changes fastest.
Arguments:
- queries: bfloat16 [65536, 512], P('seq', 'head'), may hold values from -60 to 60
- key_vectors: bfloat16 [65536, 512], P('seq', 'head'), may hold values from -6 to 6
- value_vectors: bfloat16 [65536, 512], P('seq', 'head'), may hold values from -6 to 6
- out_grad: bfloat16 [65536, 512], P('seq', 'head'), may hold values from -6 to 6
- out_weight: bfloat16 [512, 512], P('head'), may hold values from -0.25 to 0.25
- mid_keep: int32 [256, 48], P('seq'), may hold values 0 or 1
- frame_keep: int32 [256], P('seq'), may hold values from 0 to 1, as said below
Outputs:
- output: bfloat16 [65536, 512], P('seq', 'head')
- query_gradient: bfloat16 [65536, 512], P('seq', 'head')
- key_gradient: bfloat16 [65536, 512], P('seq', 'head')
- value_gradient: bfloat16 [65536, 512], P('seq', 'head')
- weight_grad: float32 [512, 512], P('head')
The draws below stay inside these ranges and needn't reach their ends.
Inputs may be any that keep to these rules, and one draw needn't show every extreme that they name: `frame_keep`: frame boundaries fall only inside shards: the first near block of every shard of 512 tokens holds 1.
All inputs are finite; a program needn't handle non-finite values. No bound on the sum of `mid_keep` on one device may be relied on, other than what follows from the above.
Results may differ from the reference program's by a relative error of at most 0.0057.
The reference program's roundings to bfloat16 on the way count: a program that leaves them out, or rounds other values in their place, can miss the bound.
Values may be sent and summed in bfloat16 or wider, within the bound.
A program may use at most 64 MiB of HBM per device.

```python
import math
import jax
import jax.numpy as jnp
from jax import lax

HEADS = 8
HDIM = 64
FEAT = 512
TOK_DEV = 512
NEAR = 256
MIDG = 8
FARG = 128
REACH = 12
TOKENS = 65536
MWIDTH = 48


def shared_keys(key):
    key_table = jnp.clip(jax.random.normal(jax.random.fold_in(key, 104), (TOKENS, FEAT), jnp.float32), -6.0, 6.0)
    return key_table


def draw_key_vectors(key, part):
    return shared_keys(key).astype(jnp.bfloat16)


def draw_queries(key, part):
    result = jnp.clip(2.5 * jax.random.normal(jax.random.fold_in(key, 106), (TOKENS, FEAT), jnp.float32), -15.0, 15.0)
    return result.astype(jnp.bfloat16)


def draw_frame_keep(key, part):
    block_count = TOKENS // NEAR
    draws = jax.random.randint(jax.random.fold_in(key, 107), (block_count,), 0, 4, dtype=jnp.int32)
    block_ids = jnp.arange(block_count, dtype=jnp.int32)
    opening = block_ids % (TOK_DEV // NEAR) == 0
    return jnp.where(opening, 1, (draws > 0).astype(jnp.int32)).astype(jnp.int32)


def touch_ends(array, stream_key, least, largest):
    index_at = [jax.random.randint(jax.random.fold_in(stream_key, axis), (), 0, length) for axis, length in enumerate(array.shape)]
    longest = array.shape.index(max(array.shape))
    beside = index_at[:longest] + [(index_at[longest] + 1) % array.shape[longest]] + index_at[longest + 1:]
    return array.at[tuple(index_at)].set(least).at[tuple(beside)].set(largest)


def block_scale(key, dims, split, smallest, top_value):
    loudness = 1.0
    for position, blocks in split:
        steps = jax.random.uniform(jax.random.fold_in(jax.random.fold_in(key, 6), position), (blocks,), jnp.float32, smallest / len(split), top_value / len(split))
        loudness = loudness * jnp.repeat(jnp.exp(steps), dims[position] // blocks).reshape((-1,) + (1,) * (len(dims) - 1 - position))
    return loudness


def noise(key, extent, scale, most, cuts=(), kind=jnp.bfloat16):
    drawn = jax.random.normal(key, extent, jnp.float32) * scale
    if len(cuts) > 0:
        drawn = block_scale(key, extent, cuts, -0.22, 0.18) * drawn
    return jnp.clip(drawn, min=-most, max=most).astype(kind)


def setup_inputs(seed: int = 0) -> dict:
    keys = jax.random.split(jax.random.key(seed), 8)
    return {
        "queries": draw_queries(jax.random.fold_in(keys[7], 71), 0),
        "key_vectors": draw_key_vectors(jax.random.fold_in(keys[7], 71), 0),
        "value_vectors": noise(keys[2], (TOKENS, FEAT), 1.0, 6.0, ((0, 128), (1, 2))),
        "out_grad": noise(keys[3], (TOKENS, FEAT), 1.0, 6.0, ((0, 128), (1, 2))),
        "out_weight": noise(keys[4], (FEAT, FEAT), FEAT ** -0.5, 0.25, ((0, 2),)),
        "mid_keep": touch_ends((jax.random.randint(keys[5], (TOKENS // NEAR, MWIDTH), 0, 4) < 3).astype(jnp.int32), jax.random.fold_in(keys[5], 1), 0, 1),
        "frame_keep": draw_frame_keep(jax.random.fold_in(keys[7], 71), 0),
    }


def pooled(source, stride, rooted):
    total = source.astype(jnp.float32).reshape(-1, stride, source.shape[1]).sum(axis=1)
    divisor = math.sqrt(stride) if rooted else float(stride)
    return (total / divisor).astype(jnp.bfloat16)

def visibility(block_id, device_id, length, frame_flag, keep_row, coarse_count):
    query_pos = block_id * NEAR + jnp.arange(NEAR, dtype=jnp.int32)[:, None]
    near_pos = (block_id - 1) * NEAR + jnp.arange(2 * NEAR, dtype=jnp.int32)[None, :]
    near_seen = (near_pos <= query_pos) & (near_pos >= 0) & ((near_pos >= block_id * NEAR) | (frame_flag == 1))
    groups = length // MIDG
    starts = ((device_id - REACH) * groups + jnp.arange(REACH * groups, dtype=jnp.int32)) * MIDG
    kept = jnp.repeat(keep_row, FARG // MIDG) == 1
    middle_seen = (starts >= 0) & (starts + MIDG <= (block_id - 1) * NEAR) & kept
    far_seen = (jnp.arange(coarse_count, dtype=jnp.int32) + 1) * FARG <= (block_id - 1) * NEAR
    columns = jnp.concatenate([middle_seen, far_seen])
    return jnp.concatenate([near_seen, jnp.broadcast_to(columns[None, :], (NEAR, columns.shape[0]))], axis=1)

def attend(query_tile, key_tile, value_tile, visible, gradient_tile, scale_amount):
    query_float = query_tile.astype(jnp.float32)
    key_float = key_tile.astype(jnp.float32)
    value_float = value_tile.astype(jnp.float32)
    gradient_float = gradient_tile.astype(jnp.float32)
    logit_matrix = jnp.einsum('aos,ros->oar', query_float, key_float) * scale_amount
    logit_matrix = jnp.where(visible[None], logit_matrix, -1e+30)
    row_top = lax.optimization_barrier(jnp.max(logit_matrix, axis=2, keepdims=True))
    weights = jnp.exp(logit_matrix - row_top)
    shares = weights / lax.optimization_barrier(jnp.sum(weights, axis=2, keepdims=True))
    rounded_scores = shares.astype(jnp.bfloat16)
    mixed_result = jnp.einsum('svu,usc->vsc', rounded_scores.astype(jnp.float32), value_float).astype(jnp.bfloat16)
    shared_gradient = jnp.einsum('aos,ros->oar', gradient_float, value_float)
    centre = lax.optimization_barrier(jnp.sum(shares * shared_gradient, axis=2, keepdims=True))
    decay_slopes = (shares * (shared_gradient - centre)).astype(jnp.bfloat16).astype(jnp.float32)
    query_gradient = jnp.einsum('svu,usc->vsc', decay_slopes, key_float) * scale_amount
    key_gradient = jnp.einsum('equ,qeb->ueb', decay_slopes, query_float) * scale_amount
    value_gradient = jnp.einsum('equ,qeb->ueb', rounded_scores.astype(jnp.float32), gradient_float)
    return (mixed_result, query_gradient, key_gradient, value_gradient)

def slab(source, start, size):
    return lax.dynamic_slice_in_dim(source, start, size, 0)

def shaped(block_rows):
    return block_rows.reshape(block_rows.shape[0], HEADS, HDIM)

def reference(queries, key_vectors, value_vectors, out_grad, out_weight, mid_keep, frame_keep):
    scale_amount = HDIM ** (-0.5)
    device_blocks = TOK_DEV // NEAR
    groups = TOK_DEV // MIDG
    window_rows = REACH * groups
    coarse_count = TOKENS // FARG
    mixed_grad = jnp.dot(out_grad, out_weight.T, preferred_element_type=jnp.float32).astype(jnp.bfloat16)
    middle_keys = pooled(key_vectors, MIDG, True)
    middle_values = pooled(value_vectors, MIDG, False)
    coarse_keys = pooled(key_vectors, FARG, True)
    coarse_values = pooled(value_vectors, FARG, False)
    near_keys = jnp.concatenate([jnp.zeros((NEAR, FEAT), jnp.bfloat16), key_vectors], axis=0)
    near_values = jnp.concatenate([jnp.zeros((NEAR, FEAT), jnp.bfloat16), value_vectors], axis=0)
    front = jnp.zeros((REACH * groups, FEAT), jnp.bfloat16)
    padded_keys = jnp.concatenate([front, middle_keys], axis=0)
    padded_values = jnp.concatenate([front, middle_values], axis=0)

    def visit(carry, block_id):
        near_kg, near_vg, middle_kg, middle_vg, coarse_kg, coarse_vg = carry
        device_id = block_id // device_blocks
        head_row = block_id * NEAR
        window_row = device_id * groups
        key_tile = jnp.concatenate([slab(near_keys, head_row, 2 * NEAR), slab(padded_keys, window_row, window_rows), coarse_keys], axis=0)
        value_tile = jnp.concatenate([slab(near_values, head_row, 2 * NEAR), slab(padded_values, window_row, window_rows), coarse_values], axis=0)
        visible = visibility(block_id, device_id, TOK_DEV, frame_keep[block_id], mid_keep[block_id], coarse_count)
        mixed_result, query_part, key_part, value_part = attend(shaped(slab(queries, head_row, NEAR)), shaped(key_tile), shaped(value_tile), visible, shaped(slab(mixed_grad, head_row, NEAR)), scale_amount)
        key_part = key_part.reshape(-1, FEAT)
        value_part = value_part.reshape(-1, FEAT)
        near_kg = lax.dynamic_update_slice_in_dim(near_kg, slab(near_kg, head_row, 2 * NEAR) + key_part[:2 * NEAR], head_row, 0)
        near_vg = lax.dynamic_update_slice_in_dim(near_vg, slab(near_vg, head_row, 2 * NEAR) + value_part[:2 * NEAR], head_row, 0)
        middle_kg = lax.dynamic_update_slice_in_dim(middle_kg, slab(middle_kg, window_row, window_rows) + key_part[2 * NEAR:2 * NEAR + window_rows], window_row, 0)
        middle_vg = lax.dynamic_update_slice_in_dim(middle_vg, slab(middle_vg, window_row, window_rows) + value_part[2 * NEAR:2 * NEAR + window_rows], window_row, 0)
        coarse_kg = coarse_kg + key_part[2 * NEAR + window_rows:]
        coarse_vg = coarse_vg + value_part[2 * NEAR + window_rows:]
        return ((near_kg, near_vg, middle_kg, middle_vg, coarse_kg, coarse_vg), (mixed_result.reshape(NEAR, FEAT), query_part.reshape(NEAR, FEAT)))
    start_state = (jnp.zeros((NEAR + TOKENS, FEAT), jnp.float32), jnp.zeros((NEAR + TOKENS, FEAT), jnp.float32), jnp.zeros((REACH * groups + TOKENS // MIDG, FEAT), jnp.float32), jnp.zeros((REACH * groups + TOKENS // MIDG, FEAT), jnp.float32), jnp.zeros((coarse_count, FEAT), jnp.float32), jnp.zeros((coarse_count, FEAT), jnp.float32))
    final_state, stacked = lax.scan(visit, start_state, jnp.arange(TOKENS // NEAR, dtype=jnp.int32))
    near_kg, near_vg, middle_kg, middle_vg, coarse_kg, coarse_vg = final_state
    attention = stacked[0].reshape(TOKENS, FEAT)
    query_gradient = stacked[1].reshape(TOKENS, FEAT).astype(jnp.bfloat16)
    key_gradient = near_kg[NEAR:] + jnp.repeat(middle_kg[REACH * groups:], MIDG, axis=0) / math.sqrt(MIDG) + jnp.repeat(coarse_kg, FARG, axis=0) / math.sqrt(FARG)
    value_gradient = near_vg[NEAR:] + jnp.repeat(middle_vg[REACH * groups:], MIDG, axis=0) / MIDG + jnp.repeat(coarse_vg, FARG, axis=0) / FARG
    output = jnp.dot(attention, out_weight, preferred_element_type=jnp.float32).astype(jnp.bfloat16)
    weight_grad = jnp.dot(attention.T, out_grad, preferred_element_type=jnp.float32) / math.sqrt(TOKENS)
    return (output, query_gradient, key_gradient.astype(jnp.bfloat16), value_gradient.astype(jnp.bfloat16), weight_grad)
```

```python
import math
import jax, jax.numpy as jnp
from jax import lax
from jax.experimental import pallas as pl
from jax.experimental.pallas import tpu as pltpu
from jax.sharding import Mesh
from jax.sharding import PartitionSpec as P

F32, BF16 = jnp.float32, jnp.bfloat16
VM = pl.BlockSpec(memory_space=pltpu.VMEM)
SM = pl.BlockSpec(memory_space=pltpu.SMEM)
NEG = -1e30
MIDG = 8
FARG = 128


def dot(a, b):
    return lax.dot_general(a, b, (((1,), (0,)), ((), ())), preferred_element_type=F32)


def dot_nt(a, b):
    return lax.dot_general(a, b, (((1,), (1,)), ((), ())), preferred_element_type=F32)


def fold(x, op):
    return op(x.reshape(x.shape[0] // 8, 8, x.shape[1]), axis=0)


def attention_kernel(q_ref, k_ref, v_ref, g_ref, go_ref, w_ref, rim_ref, win_ref, coarse_ref, keep_ref, frame_ref,
                     att_ref, dq_ref, near_ref, rimg_ref, wing_ref, coarseg_ref, wg_ref,
                     mixed, kaug, vcat, kt, vt, sbuf, dbuf, grads, attT, dqT, qaugT, gT, qm, gm):
    at_ = Place()
    g, s_own, h = at_.plane, at_.shard, at_.h
    p = 4 * g + s_own
    mine = pl.multiple_of(h * 256, 256)
    other = pl.multiple_of((1 - h) * 256, 256)
    mixed[...] = (dot_nt(g_ref[...], w_ref[:, pl.ds(mine, 256)]) + dot_nt(go_ref[...], w_ref[:, pl.ds(other, 256)])).astype(BF16)

    lane = lax.broadcasted_iota(jnp.int32, (16, 128), 1)

    def tile(bias0, bias1):
        return jnp.where(lane == 0, bias0, jnp.where(lane == 1, bias1, 0.0)).astype(BF16)

    def shut(seen):
        return jnp.where(seen, 0.0, NEG).astype(F32)

    first = tile(shut((frame_ref[0] == 1) & (p > 0)), jnp.float32(0.0))
    second = tile(jnp.float32(0.0), shut(frame_ref[1] == 1))
    third = tile(jnp.float32(0.0), jnp.float32(0.0))
    for t in range(16):
        kaug[0, 16 * t:16 * t + 16, 128:256] = first
        kaug[1, 16 * t:16 * t + 16, 128:256] = second
        kaug[2, 16 * t:16 * t + 16, 128:256] = third
    for slot in range(3):
        for k in range(4):
            j = 2 * (k % 2) + k // 2
            at = lax.rem(4 * slot + j - s_own + 12, 12)
            real = p - 12 + at >= 0
            for r in range(4):
                w0 = keep_ref[0, 4 * at + r] == 1
                w1 = keep_ref[1, 4 * at + r] == 1
                if r >= 2:
                    w0 = w0 & (at < 11)
                row = 64 * k + 16 * r
                kaug[3 + slot, row:row + 16, 128:256] = tile(shut(w0 & real), shut(w1 & real))
    rows = lax.broadcasted_iota(jnp.int32, (256, 128), 0)
    lanes = lax.broadcasted_iota(jnp.int32, (256, 128), 1)
    for half in range(2):
        limit = 2 * (2 * p - 1) - 256 * half + 2 * lanes
        kaug[6 + half, :, 128:256] = jnp.where((lanes < 2) & (rows >= limit), NEG, 0.0).astype(BF16)

    @pl.loop(0, 2)
    def _(r):
        lo = pl.multiple_of(r * 128, 128)
        hi = pl.multiple_of(256 + r * 128, 128)
        for ci in range(8):
            if ci == 0:
                kk, vv = rim_ref[:, pl.ds(lo, 128)], rim_ref[:, pl.ds(hi, 128)]
            elif ci < 3:
                kk = k_ref[256 * (ci - 1):256 * ci, pl.ds(lo, 128)]
                vv = v_ref[256 * (ci - 1):256 * ci, pl.ds(lo, 128)]
            elif ci < 6:
                kk = win_ref[256 * (ci - 3):256 * (ci - 2), pl.ds(lo, 128)]
                vv = win_ref[256 * (ci - 3):256 * (ci - 2), pl.ds(hi, 128)]
            else:
                kk = coarse_ref[256 * (ci - 6):256 * (ci - 5), pl.ds(lo, 128)]
                vv = coarse_ref[256 * (ci - 6):256 * (ci - 5), pl.ds(hi, 128)]
            kaug[ci, :, 0:128] = kk
            vcat[ci] = vv
            kt[ci] = kk.T
            vt[ci] = vv.T
        sub = lax.broadcasted_iota(jnp.int32, (128, 256), 0)
        lan = lax.broadcasted_iota(jnp.int32, (256, 128), 1)
        subq = lax.broadcasted_iota(jnp.int32, (128, 512), 0)
        causal_row = lax.broadcasted_iota(jnp.int32, (256, 512), 0)
        causal_q = lax.broadcasted_iota(jnp.int32, (256, 512), 1) % 256
        zero = jnp.zeros((), BF16)
        for b in range(2):
            qp = q_ref[256 * b:256 * b + 256, pl.ds(lo, 128)] * jnp.asarray(0.125, BF16)
            gp = mixed[256 * b:256 * b + 256, pl.ds(lo, 128)]
            qt, gt = qp.T, gp.T
            for head in range(2):
                keep_t = (sub // 64) == head
                keep_l = (lan // 64) == head
                qaugT[0:128, 256 * head:256 * head + 256] = jnp.where(keep_t, qt, zero)
                gT[:, 256 * head:256 * head + 256] = jnp.where(keep_t, gt, zero)
                qm[256 * head:256 * head + 256, :] = jnp.where(keep_l, qp, zero)
                gm[256 * head:256 * head + 256, :] = jnp.where(keep_l, gp, zero)
            qaugT[128:256, :] = jnp.where(subq == b, 1.0, 0.0).astype(BF16)
            chunks = [b, b + 1, 3, 4, 5, 6, 7]
            top = jnp.full((8, 512), NEG, F32)
            for n, ci in enumerate(chunks):
                sc = dot(kaug[ci], qaugT[...])
                if n == 1:
                    sc = jnp.where(causal_row <= causal_q, sc, NEG)
                sbuf[n] = sc
                top = jnp.maximum(top, fold(sc, jnp.max))
            top = jnp.max(top, axis=0, keepdims=True)
            total = jnp.zeros((8, 512), F32)
            centre = jnp.zeros((8, 512), F32)
            for n, ci in enumerate(chunks):
                e = jnp.exp(sbuf[n] - top)
                dp = dot(vcat[ci], gT[...])
                sbuf[n] = e
                dbuf[n] = dp
                total = total + fold(e, jnp.sum)
                centre = centre + fold(e * dp, jnp.sum)
            inv = 1.0 / jnp.sum(total, axis=0, keepdims=True)
            centre = jnp.sum(centre, axis=0, keepdims=True) * inv
            oT = [jnp.zeros((64, 256), F32)] * 2
            qT = [jnp.zeros((64, 256), F32)] * 2
            for n, ci in enumerate(chunks):
                share = sbuf[n] * inv
                pr = share.astype(BF16)
                ds = (share * (dbuf[n] - centre)).astype(BF16)
                dk = dot(ds, qm[...])
                dv = dot(pr, gm[...])
                if b == 1 and ci != 2:
                    grads[ci, :, 0:128] += dk
                    grads[ci, :, 128:256] += dv
                else:
                    grads[ci, :, 0:128] = dk
                    grads[ci, :, 128:256] = dv
                for head in range(2):
                    oT[head] = oT[head] + dot(vt[ci, 64 * head:64 * head + 64, :], pr[:, 256 * head:256 * head + 256])
                    qT[head] = qT[head] + dot(kt[ci, 64 * head:64 * head + 64, :], ds[:, 256 * head:256 * head + 256])
            for head in range(2):
                attT[r, 64 * head:64 * head + 64, 256 * b:256 * b + 256] = oT[head].astype(BF16)
                dqT[r, 64 * head:64 * head + 64, 256 * b:256 * b + 256] = (qT[head] * 0.125).astype(BF16)
        for part, where in ((0, lo), (1, hi)):
            cols = slice(128 * part, 128 * part + 128)
            rimg_ref[:, pl.ds(where, 128)] = grads[0, :, cols].astype(BF16)
            for ci in (1, 2):
                near_ref[256 * (ci - 1):256 * ci, pl.ds(where, 128)] = grads[ci, :, cols]
            for ci in (3, 4, 5):
                wing_ref[256 * (ci - 3):256 * (ci - 2), pl.ds(where, 128)] = grads[ci, :, cols].astype(BF16)
            for ci in (6, 7):
                coarseg_ref[256 * (ci - 6):256 * (ci - 5), pl.ds(where, 128)] = grads[ci, :, cols].astype(BF16)
        att_ref[:, pl.ds(lo, 128)] = attT[r].T
        dq_ref[:, pl.ds(lo, 128)] = dqT[r].T

    scale = 1.0 / 256.0
    at = attT[...].reshape(256, 512)
    wg_ref[:, pl.ds(mine, 256)] = (dot(at, g_ref[...]) * scale).astype(BF16)
    wg_ref[:, pl.ds(other, 256)] = (dot(at, go_ref[...]) * scale).astype(BF16)


def attention(*args):
    return pl.pallas_call(
        attention_kernel,
        out_shape=[
            jax.ShapeDtypeStruct((512, 256), BF16), jax.ShapeDtypeStruct((512, 256), BF16),
            jax.ShapeDtypeStruct((512, 512), F32), jax.ShapeDtypeStruct((256, 512), BF16),
            jax.ShapeDtypeStruct((768, 512), BF16), jax.ShapeDtypeStruct((512, 512), BF16),
            jax.ShapeDtypeStruct((256, 512), BF16)],
        in_specs=[VM] * 9 + [SM] * 2,
        out_specs=[VM] * 7,
        scratch_shapes=[
            pltpu.VMEM((512, 256), BF16), pltpu.VMEM((8, 256, 256), BF16), pltpu.VMEM((8, 256, 128), BF16),
            pltpu.VMEM((8, 128, 256), BF16), pltpu.VMEM((8, 128, 256), BF16),
            pltpu.VMEM((7, 256, 512), F32), pltpu.VMEM((7, 256, 512), F32), pltpu.VMEM((8, 256, 256), F32),
            pltpu.VMEM((2, 128, 512), BF16), pltpu.VMEM((2, 128, 512), BF16),
            pltpu.VMEM((256, 512), BF16), pltpu.VMEM((128, 512), BF16),
            pltpu.VMEM((512, 128), BF16), pltpu.VMEM((512, 128), BF16)],
        compiler_params=pltpu.CompilerParams(vmem_limit_bytes=48 * 2**20),
        name="attention",
    )(*args)


MESH = pl.DeviceIdType.MESH


class Place:
    def __init__(self):
        self.x, self.z = lax.axis_index("x"), lax.axis_index("z")
        self.yh, self.c, self.h = lax.axis_index("yh"), lax.axis_index("c"), lax.axis_index("h")
        self.plane = 8 * self.x + self.z
        self.shard = 2 * self.yh + self.c
        self.core = {"c": 1 - self.c}
        self.far = {"yh": 1 - self.yh}
        self.diagonal = {"yh": 1 - self.yh, "c": 1 - self.c}
        self.head = {"h": 1 - self.h}

    def along_z(self, i):
        return lax.rem(self.z + i, 8)

    def along_x(self, i):
        return lax.rem(self.x + i, 4)

    def next_plane(self, step):
        to = lax.rem(self.plane + step + 32, 32)
        return {"x": to // 8, "z": lax.rem(to, 8)}

    def next_shard(self, step):
        to = lax.rem(4 * self.plane + self.shard + step + 128, 128)
        return {"x": to // 32, "z": lax.rem(to // 4, 8), "yh": lax.rem(to // 2, 2), "c": lax.rem(to, 2)}

    def greet(self, diagonal):
        peers = [self.core, self.far, self.head, self.next_plane(1), self.next_plane(-1), self.next_shard(1), self.next_shard(-1)]
        peers += [{"z": self.along_z(i)} for i in range(1, 8)]
        peers += [{"x": self.along_x(i)} for i in range(1, 4)]
        if diagonal:
            peers.append(self.diagonal)
        barrier = pltpu.get_barrier_semaphore()
        for peer in peers:
            pl.semaphore_signal(barrier, inc=1, device_id=peer, device_id_type=MESH)
        return barrier, len(peers)


class Mail:
    def __init__(self, send_sems, recv_sems):
        self.sems, self.used, self.all = (send_sems, recv_sems), 0, []

    def send(self, source, target, device):
        at = self.used
        self.used += 1
        copy = pltpu.make_async_remote_copy(
            src_ref=source, dst_ref=target, send_sem=self.sems[0].at[at], recv_sem=self.sems[1].at[at],
            device_id=device, device_id_type=MESH)
        copy.start()
        self.all.append(copy)
        return copy

    def finish(self):
        for copy in self.all:
            copy.wait_send()


def gather_kernel(k_ref, v_ref, g_ref, w_ref, rim_ref, win_ref, coarse_ref, go_ref, wo_ref, pooled, last, send_sems, recv_sems):
    at = Place()
    barrier, count = at.greet(False)
    row = lax.broadcasted_iota(jnp.int32, (80, 512), 0)
    token = lax.broadcasted_iota(jnp.int32, (80, 512), 1)
    group = jnp.where(row < 64, token // MIDG, 128 + token // FARG)
    owner = jnp.where(row < 64, row, 128 + (row - 64) - 4 * at.shard)
    ones = jnp.where(owner == group, 1.0, 0.0).astype(BF16)
    kind = lax.broadcasted_iota(jnp.int32, (80, 256), 0)
    me = 2 * at.c + at.yh
    pooled[me, :, 0:256] = (dot(ones, k_ref[...]) / jnp.where(kind < 64, math.sqrt(MIDG), math.sqrt(FARG))).astype(BF16)
    pooled[me, :, 256:512] = (dot(ones, v_ref[...]) / jnp.where(kind < 64, float(MIDG), float(FARG))).astype(BF16)
    pl.semaphore_wait(barrier, count)

    mail = Mail(send_sems, recv_sems)
    pair = pl.ds(2 * at.c, 2)
    far = mail.send(pooled.at[me], pooled.at[me], at.far)
    rim = [mail.send(k_ref.at[256:512, :], rim_ref.at[:, 0:256], at.next_shard(1)),
           mail.send(v_ref.at[256:512, :], rim_ref.at[:, 256:512], at.next_shard(1))]
    heads = [mail.send(g_ref, go_ref, at.head),
             mail.send(w_ref.at[:, pl.ds(pl.multiple_of(256 * (1 - at.h), 256), 256)], wo_ref, at.head)]
    far.wait_recv()
    beside = mail.send(pooled.at[pair], pooled.at[pair], at.core)
    ahead = at.next_plane(1)
    hop1 = mail.send(pooled.at[pair, 0:64, :], win_ref.at[2, pair], ahead)
    beside.wait_recv()
    half = pl.ds(pl.multiple_of(256 * at.c, 256), 256)
    total = pooled[0, 64:80, half].astype(F32)
    for n in range(1, 4):
        total = total + pooled[n, 64:80, half].astype(F32)
    coarse_ref[at.plane, :, half] = total.astype(BF16)
    mine = coarse_ref.at[at.plane, :, half]
    over_z = [mail.send(mine, mine, {"z": at.along_z(i)}) for i in range(1, 8)]
    hop1.wait_recv()
    hop2 = mail.send(win_ref.at[2, pair], win_ref.at[1, pair], ahead)
    share1 = mail.send(win_ref.at[2, pair], win_ref.at[2, pair], at.core)
    for copy in over_z:
        copy.wait_recv()
    line = coarse_ref.at[pl.ds(8 * at.x, 8), :, half]
    over_x = [mail.send(line, line, {"x": at.along_x(i)}) for i in range(1, 4)]
    hop2.wait_recv()
    hop3 = mail.send(win_ref.at[1, pair], last.at[pair], ahead)
    share2 = mail.send(win_ref.at[1, pair], win_ref.at[1, pair], at.core)
    for copy in over_x:
        copy.wait_recv()
    whole = coarse_ref.at[:, :, half]
    share_coarse = mail.send(whole, whole, at.core)
    hop3.wait_recv()
    share3 = mail.send(last.at[pair], last.at[pair], at.core)
    share3.wait_recv()
    for n in range(4):
        old = 2 * (n % 2) + n // 2 >= at.shard
        win_ref[0, n] = jnp.where(old, last[n], pooled[n, 0:64, :])
    for copy in [share1, share2, share_coarse] + rim + heads:
        copy.wait_recv()
    mail.finish()


def gather(k, v, g, w):
    return pl.pallas_call(
        gather_kernel,
        out_shape=[
            jax.ShapeDtypeStruct((256, 512), BF16), jax.ShapeDtypeStruct((3, 4, 64, 512), BF16),
            jax.ShapeDtypeStruct((32, 16, 512), BF16), jax.ShapeDtypeStruct((512, 256), BF16),
            jax.ShapeDtypeStruct((256, 256), BF16)],
        in_specs=[VM] * 4,
        out_specs=[VM] * 5,
        scratch_shapes=[
            pltpu.VMEM((4, 80, 512), BF16), pltpu.VMEM((4, 64, 512), BF16),
            pltpu.SemaphoreType.DMA((23,)), pltpu.SemaphoreType.DMA((23,))],
        compiler_params=pltpu.CompilerParams(collective_id=0, has_side_effects=True, vmem_limit_bytes=32 * 2**20),
        name="gather",
    )(k, v, g, w)


def reduce_kernel(att_ref, near_ref, rimg_ref, wing_ref, cg_ref, wg_ref, w_ref, wo_ref,
                  out_ref, kg_ref, vg_ref, weight_ref,
                  atto, rimr, winr, coarser, wgr, wx, wxr, wz, wzr, wfar, wmine, wall, cx, cxr, cz, czr, cp, cpr, cfull,
                  acc, hops, hopr, midb, midr, send_sems, recv_sems):
    at = Place()
    barrier, count = at.greet(True)
    pl.semaphore_wait(barrier, count)
    mail = Mail(send_sems, recv_sems)
    c, x, z, yh = at.c, at.x, at.z, at.yh

    def lanes(n):
        return pl.ds(pl.multiple_of(256 * n, 256), 256)

    def up(value):
        return value.astype(F32)

    to_w = mail.send(wg_ref.at[pl.ds(pl.multiple_of(128 * (1 - c), 128), 128), :], wgr, at.core)
    to_win = mail.send(wing_ref.at[:, pl.ds(2 * (1 - c), 2)], winr, at.core)
    to_c = mail.send(cg_ref.at[:, :, lanes(1 - c)], coarser, at.core)
    to_att = mail.send(att_ref, atto, at.head)
    to_rim = mail.send(rimg_ref, rimr, at.next_shard(-1))

    to_w.wait_recv()
    wx[...] = (up(wg_ref[pl.ds(pl.multiple_of(128 * c, 128), 128), :]) + up(wgr[...])).astype(BF16).reshape(4, 32, 512)
    to_wx = [mail.send(wx.at[at.along_x(i)], wxr.at[i - 1], {"x": at.along_x(i)}) for i in range(1, 4)]

    to_win.wait_recv()
    shard, beside = at.shard, 2 * yh + 1 - c
    for n in range(2):
        j = 2 * n + c
        own, got = up(wing_ref[0, 2 * c + n]), up(winr[0, n])
        hops[0, n] = (jnp.where(j >= shard, own, 0.0) + jnp.where(j >= beside, got, 0.0)).astype(BF16)
        acc[2, n] = jnp.where(j >= shard, 0.0, own) + jnp.where(j >= beside, 0.0, got)
    back = at.next_plane(-1)
    hop = [mail.send(hops.at[0], hopr.at[0], back)]
    for m in range(2):
        acc[m] = up(wing_ref[1 + m, pl.ds(2 * c, 2)]) + up(winr[1 + m])

    to_c.wait_recv()
    cx[...] = (up(cg_ref[:, :, lanes(c)]) + up(coarser[...])).astype(BF16)
    to_cx = [mail.send(cx.at[pl.ds(8 * at.along_x(i), 8)], cxr.at[i - 1], {"x": at.along_x(i)}) for i in range(1, 4)]

    for copy in to_wx:
        copy.wait_recv()
    total = up(wx[x])
    for i in range(3):
        total = total + up(wxr[i])
    for n in range(8):
        wz[n] = total[16 * (n // 4):16 * (n // 4) + 16, 128 * (n % 4):128 * (n % 4) + 128].astype(BF16)
    to_wz = [mail.send(wz.at[at.along_z(i)], wzr.at[i - 1], {"z": at.along_z(i)}) for i in range(1, 8)]

    for copy in to_cx:
        copy.wait_recv()
    total = up(cx[pl.ds(8 * x, 8)])
    for i in range(3):
        total = total + up(cxr[i])
    cz[...] = total.astype(BF16)
    to_cz = [mail.send(cz.at[at.along_z(i)], czr.at[i - 1], {"z": at.along_z(i)}) for i in range(1, 8)]

    hop[0].wait_recv()
    hops[1] = (up(hopr[0]) + acc[0]).astype(BF16)
    hop.append(mail.send(hops.at[1], hopr.at[1], back))

    for copy in to_wz:
        copy.wait_recv()
    total = up(wz[z])
    for i in range(7):
        total = total + up(wzr[i])
    wmine[...] = total
    to_far = mail.send(wmine, wfar, at.far)

    for copy in to_cz:
        copy.wait_recv()
    total = up(cz[z])
    for i in range(7):
        total = total + up(czr[i])
    cp[...] = total.astype(BF16)
    to_cp = [mail.send(cp, cpr.at[n], peer) for n, peer in enumerate((at.far, at.core, at.diagonal))]

    hop[1].wait_recv()
    hops[2] = (up(hopr[1]) + acc[1]).astype(BF16)
    hop.append(mail.send(hops.at[2], hopr.at[2], back))

    to_far.wait_recv()
    wall[z] = wmine[...] + wfar[...]
    to_wall = [mail.send(wall.at[z], wall.at[z], {"z": at.along_z(i)}) for i in range(1, 8)]

    to_att.wait_recv()
    out_ref[...] = (dot(att_ref[...], w_ref[:, lanes(at.h)]) + dot(atto[...], wo_ref[...])).astype(BF16)

    for copy in to_wall:
        copy.wait_recv()
    for n in range(8):
        weight_ref[c, x, 16 * (n // 4):16 * (n // 4) + 16, 128 * (n % 4):128 * (n % 4) + 128] = wall[n]
    line = weight_ref.at[c, x]
    to_line = [mail.send(line, line, {"x": at.along_x(i)}) for i in range(1, 4)]

    hop[2].wait_recv()
    acc[0] = up(hopr[2]) + acc[2]
    midb[...] = acc[0, 1 - yh].astype(BF16)
    to_mid = mail.send(midb, midr, at.far)

    for copy in to_cp:
        copy.wait_recv()
    cfull[:, lanes(c)] = up(cp[...]) + up(cpr[0])
    cfull[:, lanes(1 - c)] = up(cpr[1]) + up(cpr[2])
    to_rim.wait_recv()

    for copy in to_line:
        copy.wait_recv()
    to_half = mail.send(weight_ref.at[c], weight_ref.at[c], at.core)

    to_mid.wait_recv()
    mid = acc[0, yh] + up(midr[...])
    token = lax.broadcasted_iota(jnp.int32, (512, 80), 0)
    row = lax.broadcasted_iota(jnp.int32, (512, 80), 1)
    spread = jnp.where(jnp.where(row < 64, token // MIDG, 64 + 4 * at.shard + token // FARG) == row, 1.0, 0.0).astype(BF16)
    for n, target, mid_div, far_div in ((0, kg_ref, math.sqrt(MIDG), math.sqrt(FARG)), (1, vg_ref, float(MIDG), float(FARG))):
        cols = slice(256 * n, 256 * n + 256)
        pools = jnp.concatenate([mid[:, cols] / mid_div, cfull[:, cols] / far_div], axis=0)
        high = pools.astype(BF16)
        low = (pools - up(high)).astype(BF16)
        added = dot(spread, high) + dot(spread, low) + near_ref[:, cols]
        target[0:256, :] = added[0:256].astype(BF16)
        target[256:512, :] = (added[256:512] + up(rimr[:, cols])).astype(BF16)
    to_half.wait_recv()
    mail.finish()


def reduce(att, near, rimg, wing, cg, wg, w, wo):
    B, S = (lambda *s: pltpu.VMEM(s, BF16)), (lambda *s: pltpu.VMEM(s, F32))
    return pl.pallas_call(
        reduce_kernel,
        out_shape=[
            jax.ShapeDtypeStruct((512, 256), BF16), jax.ShapeDtypeStruct((512, 256), BF16),
            jax.ShapeDtypeStruct((512, 256), BF16), jax.ShapeDtypeStruct((2, 4, 32, 512), F32)],
        in_specs=[VM] * 8,
        out_specs=[VM] * 4,
        scratch_shapes=[
            B(512, 256), B(256, 512), B(3, 2, 64, 512), B(32, 16, 256), B(128, 512),
            B(4, 32, 512), B(3, 32, 512), B(8, 16, 128), B(7, 16, 128), S(16, 128), S(16, 128), S(8, 16, 128),
            B(32, 16, 256), B(3, 8, 16, 256), B(8, 16, 256), B(7, 16, 256), B(16, 256), B(3, 16, 256), S(16, 512),
            S(3, 2, 64, 512), B(3, 2, 64, 512), B(3, 2, 64, 512), B(64, 512), B(64, 512),
            pltpu.SemaphoreType.DMA((44,)), pltpu.SemaphoreType.DMA((44,))],
        compiler_params=pltpu.CompilerParams(collective_id=1, has_side_effects=True, vmem_limit_bytes=40 * 2**20),
        name="reduce",
    )(att, near, rimg, wing, cg, wg, w, wo)


def on_device(queries, key_vectors, value_vectors, out_grad, out_weight, mid_keep, frame_keep):
    rim, win, coarse, other_grad, other_weight = gather(key_vectors, value_vectors, out_grad, out_weight)
    att, dq, near, rimg, wing, cg, wg = attention(
        queries, key_vectors, value_vectors, out_grad, other_grad, out_weight,
        rim, win.reshape(768, 512), coarse.reshape(512, 512), mid_keep, frame_keep)
    output, kg, vg, weight = reduce(
        att, near, rimg, wing.reshape(3, 4, 64, 512), cg.reshape(32, 16, 512), wg, out_weight, other_weight)
    return output, dq, kg, vg, weight.reshape(256, 512)


def solution(mesh):
    split = Mesh(mesh.devices.reshape(4, 8, 2, 2, 2), ("x", "z", "yh", "c", "h"))
    seq = ("x", "z", "yh", "c")
    return jax.shard_map(
        on_device,
        mesh=split,
        in_specs=(P(seq, "h"), P(seq, "h"), P(seq, "h"), P(seq, "h"), P("h", None), P(seq, None), P(seq)),
        out_specs=(P(seq, "h"), P(seq, "h"), P(seq, "h"), P(seq, "h"), P("h", None)),
        check_vma=False,
    )
```

```python
import math

import jax
import jax.numpy as jnp
from jax import lax
from jax.experimental import pallas as pl
from jax.experimental.pallas import tpu as pltpu
from jax.sharding import Mesh
from jax.sharding import PartitionSpec as P

F32, BF16 = jnp.float32, jnp.bfloat16
VM = pl.BlockSpec(memory_space=pltpu.VMEM)
SM = pl.BlockSpec(memory_space=pltpu.SMEM)
ANY = pl.BlockSpec(memory_space=pl.ANY)
NEG = -1e30
MIDG = 8
FARG = 128


def dot(a, b):
    return lax.dot_general(a, b, (((1,), (0,)), ((), ())), preferred_element_type=F32)


def dot_nt(a, b):
    return lax.dot_general(a, b, (((1,), (1,)), ((), ())), preferred_element_type=F32)


def fold(x, op):
    return op(x.reshape(x.shape[0] // 8, 8, x.shape[1]), axis=0)


def up(value):
    return value.astype(F32)


MESH = pl.DeviceIdType.MESH


class Place:
    def __init__(self):
        self.x, self.z = lax.axis_index("x"), lax.axis_index("z")
        self.yh, self.c, self.h = lax.axis_index("yh"), lax.axis_index("c"), lax.axis_index("h")
        self.plane = 8 * self.x + self.z
        self.shard = 2 * self.yh + self.c
        self.core = {"c": 1 - self.c}
        self.far = {"yh": 1 - self.yh}
        self.diagonal = {"yh": 1 - self.yh, "c": 1 - self.c}
        self.head = {"h": 1 - self.h}

    def along_z(self, i):
        return lax.rem(self.z + i, 8)

    def along_x(self, i):
        return lax.rem(self.x + i, 4)

    def next_plane(self, step):
        to = lax.rem(self.plane + step + 32, 32)
        return {"x": to // 8, "z": lax.rem(to, 8)}

    def next_shard(self, step):
        to = lax.rem(4 * self.plane + self.shard + step + 128, 128)
        return {"x": to // 32, "z": lax.rem(to // 4, 8), "yh": lax.rem(to // 2, 2), "c": lax.rem(to, 2)}

    def greet(self, diagonal):
        peers = [self.core, self.far, self.head, self.next_plane(1), self.next_plane(-1), self.next_shard(1), self.next_shard(-1)]
        peers += [{"z": self.along_z(i)} for i in range(1, 8)]
        peers += [{"x": self.along_x(i)} for i in range(1, 4)]
        if diagonal:
            peers.append(self.diagonal)
        barrier = pltpu.get_barrier_semaphore()
        for peer in peers:
            pl.semaphore_signal(barrier, inc=1, device_id=peer, device_id_type=MESH)
        return barrier, len(peers)


class Mail:
    def __init__(self, send_sems, recv_sems):
        self.sems, self.used, self.all = (send_sems, recv_sems), 0, []

    def send(self, source, target, device):
        at = self.used
        self.used += 1
        copy = pltpu.make_async_remote_copy(
            src_ref=source, dst_ref=target, send_sem=self.sems[0].at[at], recv_sem=self.sems[1].at[at],
            device_id=device, device_id_type=MESH)
        copy.start()
        self.all.append(copy)
        return copy

    def finish(self):
        for copy in self.all:
            copy.wait_send()


def layer_kernel(q_hbm, k_hbm, v_hbm, g_hbm, w_hbm, keep_ref, frame_ref,
                 out_ref, dq_ref, kg_ref, vg_ref, weight_ref,
                 q, k, v, g, w, rim, go, wo, pooled, win, last, coarse, mixed,
                 kaug, vcat, kt, vt, qaugT, gT, qm, gm, sbuf, dbuf, pbuf, tops, stats,
                 attT, att, atto, dqT, wg, wgb, wgr, wx, wxr, wz, wzr, wall,
                 near, rimg, rimr, wing, winr, acc, hops, hopr, mid, midb, midr,
                 cg, cr, cx, cxr, cz, czr, cp, cpr, cfull,
                 load_sems, send_sems, recv_sems):
    at = Place()
    c, x, z, yh, h, shard = at.c, at.x, at.z, at.yh, at.h, at.shard
    p = 4 * at.plane + shard
    loads = [pltpu.make_async_copy(a, b, load_sems.at[n])
             for n, (a, b) in enumerate(((k_hbm, k), (v_hbm, v), (g_hbm, g), (w_hbm, w), (q_hbm, q)))]
    for load in loads:
        load.start()
    barrier, count = at.greet(True)

    def lanes(n, size=256):
        return pl.ds(pl.multiple_of(size * n, size), size)

    row = lax.broadcasted_iota(jnp.int32, (80, 512), 0)
    token = lax.broadcasted_iota(jnp.int32, (80, 512), 1)
    owner = jnp.where(row < 64, row, 128 + (row - 64) - 4 * shard)
    group = jnp.where(row < 64, token // MIDG, 128 + token // FARG)
    ones = jnp.where(owner == group, 1.0, 0.0).astype(BF16)
    kind = lax.broadcasted_iota(jnp.int32, (80, 256), 0)
    me, peer = 2 * c + yh, 2 * c + 1 - yh
    loads[0].wait()
    pooled[me, :, 0:256] = (dot(ones, k[...]) / jnp.where(kind < 64, math.sqrt(MIDG), math.sqrt(FARG))).astype(BF16)
    loads[1].wait()
    pooled[me, :, 256:512] = (dot(ones, v[...]) / jnp.where(kind < 64, float(MIDG), float(FARG))).astype(BF16)
    pl.semaphore_wait(barrier, count)

    mail = Mail(send_sems, recv_sems)
    ahead, back = at.next_plane(1), at.next_plane(-1)

    def relay(source, slot, place):
        target = last.at[place] if slot == 0 else win.at[slot, place]
        return mail.send(source, target, ahead)

    def share(slot, place):
        part = last.at[place] if slot == 0 else win.at[slot, place]
        return mail.send(part, part, at.core)

    hop_a1 = relay(pooled.at[me, 0:64, :], 2, me)
    far = mail.send(pooled.at[me], pooled.at[me], at.far)
    beside_a = mail.send(pooled.at[me], pooled.at[me], at.core)
    loads[2].wait()
    loads[3].wait()
    to_g = mail.send(g, go, at.head)
    to_k = mail.send(k.at[256:512, :], rim.at[:, 0:256], at.next_shard(1))
    to_v = mail.send(v.at[256:512, :], rim.at[:, 256:512], at.next_shard(1))
    to_wo = mail.send(w.at[:, lanes(1 - h)], wo, at.head)

    lane = lax.broadcasted_iota(jnp.int32, (16, 128), 1)

    def tile(bias0, bias1):
        return jnp.where(lane == 0, bias0, jnp.where(lane == 1, bias1, 0.0)).astype(BF16)

    def shut(seen):
        return jnp.where(seen, 0.0, NEG).astype(F32)

    def put(ci, at_row, value):
        for r in range(2):
            kaug[r, ci, at_row:at_row + value.shape[0], 128:256] = value

    first = tile(shut((frame_ref[0] == 1) & (p > 0)), jnp.float32(0.0))
    second = tile(jnp.float32(0.0), shut(frame_ref[1] == 1))
    for t in range(16):
        put(0, 16 * t, first)
        put(1, 16 * t, second)
    put(2, 0, jnp.zeros((256, 128), BF16))
    for slot in range(3):
        for n in range(4):
            j = 2 * (n % 2) + n // 2
            index = lax.rem(4 * slot + j - shard + 12, 12)
            real = p - 12 + index >= 0
            for r in range(4):
                keep0 = (keep_ref[0, 4 * index + r] == 1) & real
                keep1 = (keep_ref[1, 4 * index + r] == 1) & real
                if r >= 2:
                    keep0 = keep0 & (index < 11)
                put(3 + slot, 64 * n + 16 * r, tile(shut(keep0), shut(keep1)))
    rows = lax.broadcasted_iota(jnp.int32, (256, 128), 0)
    columns = lax.broadcasted_iota(jnp.int32, (256, 128), 1)
    for half in range(2):
        limit = 4 * p - 2 - 256 * half + 2 * columns
        put(6 + half, 0, jnp.where((columns < 2) & (rows >= limit), NEG, 0.0).astype(BF16))

    sub = lax.broadcasted_iota(jnp.int32, (128, 256), 0)
    subq = lax.broadcasted_iota(jnp.int32, (128, 512), 0)
    zero = jnp.zeros((), BF16)

    def by_head(source, b, r, transposed, plain):
        value = source[256 * b:256 * b + 256, 128 * r:128 * r + 128]
        turned = value.T
        for head in range(2):
            rest = slice(256 * head, 256 * head + 256)
            transposed[b, r, 0:128, rest] = jnp.where(sub // 64 == head, turned, zero)
            plain[b, r, rest, :] = jnp.where(columns // 64 == head, value, zero)

    loads[4].wait()
    q[...] = q[...] * jnp.asarray(0.125, BF16)
    for b in range(2):
        for r in range(2):
            by_head(q, b, r, qaugT, qm)
            qaugT[b, r, 128:256, :] = jnp.where(subq == b, 1.0, 0.0).astype(BF16)
            tops[b, r] = jnp.full((8, 512), NEG, F32)

    def prepare(ci):
        for r in range(2):
            lo, hi = slice(128 * r, 128 * r + 128), slice(256 + 128 * r, 384 + 128 * r)
            if ci == 0:
                kk, vv = rim[:, lo], rim[:, hi]
            elif ci < 3:
                kk, vv = k[256 * (ci - 1):256 * ci, lo], v[256 * (ci - 1):256 * ci, lo]
            elif ci < 6:
                kk, vv = win[ci - 3, :, :, lo].reshape(256, 128), win[ci - 3, :, :, hi].reshape(256, 128)
            else:
                part = slice(16 * (ci - 6), 16 * (ci - 5))
                kk, vv = coarse[part, :, lo].reshape(256, 128), coarse[part, :, hi].reshape(256, 128)
            kaug[r, ci, :, 0:128] = kk
            vcat[r, ci] = vv
            kt[r, ci] = kk.T
            vt[r, ci] = vv.T

    causal = lax.broadcasted_iota(jnp.int32, (256, 512), 0) <= lax.broadcasted_iota(jnp.int32, (256, 512), 1) % 256

    def uses(ci):
        for b in range(2):
            if ci > 2:
                yield b, ci - 1
            elif 0 <= ci - b < 2:
                yield b, ci - b

    def score(ci):
        prepare(ci)
        for r in range(2):
            for b, n in uses(ci):
                value = dot(kaug[r, ci], qaugT[b, r])
                if n == 1:
                    value = jnp.where(causal, value, NEG)
                sbuf[b, r, n] = value
                tops[b, r] = jnp.maximum(tops[b, r], fold(value, jnp.max))

    def grade(ci):
        for r in range(2):
            for b, n in uses(ci):
                dbuf[b, r, n] = dot(vcat[r, ci], gT[b, r])

    score(1)
    score(2)
    far.wait_recv()
    hop_b1 = relay(pooled.at[peer, 0:64, :], 2, peer)
    beside_b = mail.send(pooled.at[peer], pooled.at[peer], at.core)
    hop_a1.wait_recv()
    hop_a2 = relay(win.at[2, me], 1, me)
    share_a1 = share(2, me)
    beside_a.wait_recv()
    beside_b.wait_recv()
    half = lanes(c)
    total = up(pooled[0, 64:80, half])
    for n in range(1, 4):
        total = total + up(pooled[n, 64:80, half])
    coarse[at.plane, :, half] = total.astype(BF16)
    mine = coarse.at[at.plane, :, half]
    over_z = [mail.send(mine, mine, {"z": at.along_z(i)}) for i in range(1, 8)]
    hop_b1.wait_recv()
    hop_b2 = relay(win.at[2, peer], 1, peer)
    share_b1 = share(2, peer)
    hop_a2.wait_recv()
    hop_a3 = relay(win.at[1, me], 0, me)
    share_a2 = share(1, me)
    for copy in over_z:
        copy.wait_recv()
    line = coarse.at[pl.ds(8 * x, 8), :, half]
    over_x = [mail.send(line, line, {"x": at.along_x(i)}) for i in range(1, 4)]
    to_k.wait_recv()
    to_v.wait_recv()
    score(0)
    hop_b2.wait_recv()
    hop_b3 = relay(win.at[1, peer], 0, peer)
    share_b2 = share(1, peer)
    share_a1.wait_recv()
    share_b1.wait_recv()
    score(5)
    for copy in over_x:
        copy.wait_recv()
    whole = coarse.at[:, :, half]
    share_coarse = mail.send(whole, whole, at.core)
    hop_a3.wait_recv()
    share_a3 = share(0, me)
    to_g.wait_recv()
    mixed[...] = (dot_nt(g[...], w[:, lanes(h)]) + dot_nt(go[...], w[:, lanes(1 - h)])).astype(BF16)
    for b in range(2):
        for r in range(2):
            by_head(mixed, b, r, gT, gm)
    hop_b3.wait_recv()
    share_b3 = share(0, peer)
    grade(1)
    grade(2)
    share_a2.wait_recv()
    share_b2.wait_recv()
    score(4)
    share_coarse.wait_recv()
    score(6)
    score(7)
    share_a3.wait_recv()
    share_b3.wait_recv()
    for n in range(4):
        win[0, n] = jnp.where(2 * (n % 2) + n // 2 >= shard, last[n], pooled[n, 0:64, :])
    score(3)
    for ci in (0, 5, 4, 6, 7, 3):
        grade(ci)

    for r in range(2):
        for b in range(2):
            top = jnp.max(tops[b, r], axis=0, keepdims=True)
            total = jnp.zeros((8, 512), F32)
            centre = jnp.zeros((8, 512), F32)
            for n in range(7):
                e = jnp.exp(sbuf[b, r, n] - top)
                sbuf[b, r, n] = e
                total = total + fold(e, jnp.sum)
                centre = centre + fold(e * dbuf[b, r, n], jnp.sum)
            inv = 1.0 / jnp.sum(total, axis=0, keepdims=True)
            stats[b, r, 0:1] = inv
            stats[b, r, 1:2] = jnp.sum(centre, axis=0, keepdims=True) * inv
            mix = [jnp.zeros((64, 256), F32)] * 2
            for n in range(7):
                ci = n + 1 if n >= 2 else n + b
                pr = (sbuf[b, r, n] * inv).astype(BF16)
                pbuf[b, r, n] = pr
                for head in range(2):
                    mix[head] = mix[head] + dot(vt[r, ci, 64 * head:64 * head + 64, :], pr[:, 256 * head:256 * head + 256])
            for head in range(2):
                attT[r, 64 * head:64 * head + 64, 256 * b:256 * b + 256] = mix[head].astype(BF16)
        att[:, 128 * r:128 * r + 128] = attT[r].T
    to_att = mail.send(att, atto, at.head)
    turned = attT[...].reshape(256, 512)
    wg[:, lanes(h)] = dot(turned, g[...]) * (1.0 / 256.0)
    wg[:, lanes(1 - h)] = dot(turned, go[...]) * (1.0 / 256.0)
    wgb[...] = wg[pl.ds(pl.multiple_of(128 * (1 - c), 128), 128), :].astype(BF16)
    to_w = mail.send(wgb, wgr, at.core)
    for b in range(2):
        for r in range(2):
            dqT[b, r] = jnp.zeros((128, 256), F32)

    def gradients(r, ci):
        dk, dv = None, None
        for b, n in uses(ci):
            inv, centre = stats[b, r, 0:1], stats[b, r, 1:2]
            ds = (sbuf[b, r, n] * inv * (dbuf[b, r, n] - centre)).astype(BF16)
            for head in range(2):
                some = slice(64 * head, 64 * head + 64)
                dqT[b, r, some, :] += dot(kt[r, ci, some, :], ds[:, 256 * head:256 * head + 256])
            one, two = dot(ds, qm[b, r]), dot(pbuf[b, r, n], gm[b, r])
            dk, dv = (one, two) if dk is None else (dk + one, dv + two)
        for cols, value in ((slice(0, 128), dk), (slice(128, 256), dv)):
            if ci == 0:
                rimg[r, :, cols] = value.astype(BF16)
            elif ci < 3:
                near[r, 256 * (ci - 1):256 * ci, cols] = value
            elif ci < 6:
                wing[r, ci - 3, :, :, cols] = value.astype(BF16).reshape(4, 64, 128)
            else:
                cg[r, 16 * (ci - 6):16 * (ci - 5), :, cols] = value.astype(BF16).reshape(16, 16, 128)

    def finish_queries(r):
        for b in range(2):
            dq_ref[256 * b:256 * b + 256, 128 * r:128 * r + 128] = (dqT[b, r] * 0.125).astype(BF16).T

    def send_window(r):
        return mail.send(wing.at[r, :, pl.ds(2 * (1 - c), 2)], winr.at[r], at.core)

    def start_chain(r):
        beside = 2 * yh + 1 - c
        for n in range(2):
            j = 2 * n + c
            own, got = up(wing[r, 0, 2 * c + n]), up(winr[r, 0, n])
            hops[r, 0, n] = (jnp.where(j >= shard, own, 0.0) + jnp.where(j >= beside, got, 0.0)).astype(BF16)
            acc[r, 2, n] = jnp.where(j >= shard, 0.0, own) + jnp.where(j >= beside, 0.0, got)
        copy = mail.send(hops.at[r, 0], hopr.at[r, 0], back)
        for m in range(2):
            acc[r, m] = up(wing[r, 1 + m, pl.ds(2 * c, 2)]) + up(winr[r, 1 + m])
        return copy

    def go_on(r, m):
        hops[r, m] = (up(hopr[r, m - 1]) + acc[r, m - 1]).astype(BF16)
        return mail.send(hops.at[r, m], hopr.at[r, m], back)

    def end_chain(r):
        mid[r] = up(hopr[r, 2]) + acc[r, 2]
        midb[r] = mid[r, 1 - yh].astype(BF16)
        return mail.send(midb.at[r], midr.at[r], at.far)

    for ci in (3, 4, 5):
        gradients(0, ci)
    to_win0 = send_window(0)
    to_w.wait_recv()
    wx[...] = (wg[pl.ds(pl.multiple_of(128 * c, 128), 128), :] + up(wgr[...])).reshape(4, 32, 512)
    to_wx = [mail.send(wx.at[at.along_x(i)], wxr.at[i - 1], {"x": at.along_x(i)}) for i in range(1, 4)]
    gradients(0, 0)
    to_rim0 = mail.send(rimg.at[0], rimr.at[0], at.next_shard(-1))
    gradients(0, 6)
    gradients(0, 7)
    to_win0.wait_recv()
    hop_01 = start_chain(0)
    gradients(1, 6)
    gradients(1, 7)
    to_c = mail.send(cg.at[:, :, :, lanes(1 - c, 128)], cr, at.core)
    for copy in to_wx:
        copy.wait_recv()
    total = wx[x]
    for i in range(3):
        total = total + wxr[i]
    for n in range(8):
        wz[n] = total[16 * (n // 4):16 * (n // 4) + 16, 128 * (n % 4):128 * (n % 4) + 128]
    wzr[z, yh] = wz[z]
    to_wz = [mail.send(wz.at[at.along_z(i)], wzr.at[z, yh], {"z": at.along_z(i), "yh": yh if n == 0 else 1 - yh})
             for i in range(8) for n in range(2) if i + n > 0]
    gradients(1, 3)
    hop_01.wait_recv()
    hop_02 = go_on(0, 1)
    gradients(1, 4)
    gradients(1, 5)
    to_win1 = send_window(1)
    to_c.wait_recv()
    cx[...] = (up(cg[:, :, :, lanes(c, 128)]) + up(cr[...])).astype(BF16)
    to_cx = [mail.send(cx.at[:, pl.ds(8 * at.along_x(i), 8)], cxr.at[i - 1], {"x": at.along_x(i)}) for i in range(1, 4)]
    gradients(1, 0)
    to_rim1 = mail.send(rimg.at[1], rimr.at[1], at.next_shard(-1))
    to_win1.wait_recv()
    hop_11 = start_chain(1)
    hop_02.wait_recv()
    hop_03 = go_on(0, 2)
    gradients(0, 1)
    for copy in to_wz:
        copy.wait_recv()
    total = wzr[0, 0]
    for n in range(1, 16):
        total = total + wzr[n // 2, n % 2]
    wall[z] = total
    to_wall = [mail.send(wall.at[z], wall.at[z], {"z": at.along_z(i)}) for i in range(1, 8)]
    gradients(0, 2)
    finish_queries(0)
    for copy in to_cx:
        copy.wait_recv()
    total = up(cx[:, pl.ds(8 * x, 8)])
    for i in range(3):
        total = total + up(cxr[i])
    cz[...] = total.astype(BF16)
    to_cz = [mail.send(cz.at[:, at.along_z(i)], czr.at[i - 1], {"z": at.along_z(i)}) for i in range(1, 8)]
    hop_11.wait_recv()
    hop_12 = go_on(1, 1)
    hop_03.wait_recv()
    to_mid0 = end_chain(0)
    gradients(1, 1)
    for copy in to_wall:
        copy.wait_recv()
    for n in range(8):
        weight_ref[c, x, 16 * (n // 4):16 * (n // 4) + 16, 128 * (n % 4):128 * (n % 4) + 128] = wall[n]
    line = weight_ref.at[c, x]
    to_line = [mail.send(line, line, {"x": at.along_x(i)}) for i in range(1, 4)]
    gradients(1, 2)
    finish_queries(1)
    hop_12.wait_recv()
    hop_13 = go_on(1, 2)
    for copy in to_cz:
        copy.wait_recv()
    total = up(cz[:, z])
    for i in range(7):
        total = total + up(czr[i])
    cp[...] = total.astype(BF16)
    to_cp = [mail.send(cp, cpr.at[n], who) for n, who in enumerate((at.far, at.core, at.diagonal))]
    to_att.wait_recv()
    to_wo.wait_recv()
    out_ref[...] = (dot(att[...], w[:, lanes(h)]) + dot(atto[...], wo[...])).astype(BF16)
    for copy in to_line:
        copy.wait_recv()
    to_half = mail.send(weight_ref.at[c], weight_ref.at[c], at.core)
    hop_13.wait_recv()
    to_mid1 = end_chain(1)
    for copy in to_cp:
        copy.wait_recv()
    for r in range(2):
        cfull[r, :, lanes(c, 128)] = up(cp[r]) + up(cpr[0, r])
        cfull[r, :, lanes(1 - c, 128)] = up(cpr[1, r]) + up(cpr[2, r])
    token = lax.broadcasted_iota(jnp.int32, (512, 80), 0)
    row = lax.broadcasted_iota(jnp.int32, (512, 80), 1)
    spread = jnp.where(jnp.where(row < 64, token // MIDG, 64 + 4 * shard + token // FARG) == row, 1.0, 0.0).astype(BF16)
    row = lax.broadcasted_iota(jnp.int32, (80, 256), 0)
    value_lane = lax.broadcasted_iota(jnp.int32, (80, 256), 1) >= 128
    divisor = jnp.where(row < 64, jnp.where(value_lane, float(MIDG), math.sqrt(MIDG)), jnp.where(value_lane, float(FARG), math.sqrt(FARG)))
    for r, to_mid, to_rim in ((0, to_mid0, to_rim0), (1, to_mid1, to_rim1)):
        to_rim.wait_recv()
        to_mid.wait_recv()
        pools = jnp.concatenate([mid[r, yh] + up(midr[r]), cfull[r]], axis=0) / divisor
        high = pools.astype(BF16)
        low = (pools - up(high)).astype(BF16)
        added = dot(spread, high) + dot(spread, low) + near[r]
        for target, cols in ((kg_ref, slice(0, 128)), (vg_ref, slice(128, 256))):
            target[0:256, 128 * r:128 * r + 128] = added[0:256, cols].astype(BF16)
            target[256:512, 128 * r:128 * r + 128] = (added[256:512, cols] + up(rimr[r, :, cols])).astype(BF16)
    to_half.wait_recv()
    mail.finish()


def on_device(queries, key_vectors, value_vectors, out_grad, out_weight, mid_keep, frame_keep):
    B, S = (lambda *s: pltpu.VMEM(s, BF16)), (lambda *s: pltpu.VMEM(s, F32))
    T = jax.ShapeDtypeStruct((512, 256), BF16)
    output, dq, kg, vg, weight = pl.pallas_call(
        layer_kernel,
        out_shape=[T, T, T, T, jax.ShapeDtypeStruct((2, 4, 32, 512), F32)],
        in_specs=[ANY] * 5 + [SM] * 2,
        out_specs=[VM] * 5,
        scratch_shapes=[
            B(512, 256), B(512, 256), B(512, 256), B(512, 256), B(256, 512), B(256, 512), B(512, 256), B(256, 256),
            B(4, 80, 512), B(3, 4, 64, 512), B(4, 64, 512), B(32, 16, 512), B(512, 256),
            B(2, 8, 256, 256), B(2, 8, 256, 128), B(2, 8, 128, 256), B(2, 8, 128, 256),
            B(2, 2, 256, 512), B(2, 2, 128, 512), B(2, 2, 512, 128), B(2, 2, 512, 128),
            S(2, 2, 7, 256, 512), S(2, 2, 7, 256, 512), B(2, 2, 7, 256, 512), S(2, 2, 8, 512), S(2, 2, 8, 512),
            B(2, 128, 512), B(512, 256), B(512, 256), S(2, 2, 128, 256), S(256, 512), B(128, 512), B(128, 512),
            S(4, 32, 512), S(3, 32, 512), S(8, 16, 128), S(8, 2, 16, 128), S(8, 16, 128),
            S(2, 512, 256), B(2, 256, 256), B(2, 256, 256), B(2, 3, 4, 64, 256), B(2, 3, 2, 64, 256),
            S(2, 3, 2, 64, 256), B(2, 3, 2, 64, 256), B(2, 3, 2, 64, 256), S(2, 2, 64, 256), B(2, 64, 256), B(2, 64, 256),
            B(2, 32, 16, 256), B(2, 32, 16, 128), B(2, 32, 16, 128), B(3, 2, 8, 16, 128), B(2, 8, 16, 128),
            B(7, 2, 16, 128), B(2, 16, 128), B(3, 2, 16, 128), S(2, 16, 256),
            pltpu.SemaphoreType.DMA((5,)), pltpu.SemaphoreType.DMA((90,)), pltpu.SemaphoreType.DMA((90,))],
        compiler_params=pltpu.CompilerParams(collective_id=0, has_side_effects=True, vmem_limit_bytes=60 * 2**20),
        name="layer",
    )(queries, key_vectors, value_vectors, out_grad, out_weight, mid_keep, frame_keep)
    return output, dq, kg, vg, weight.reshape(256, 512)


def solution(mesh):
    split = Mesh(mesh.devices.reshape(4, 8, 2, 2, 2), ("x", "z", "yh", "c", "h"))
    seq = ("x", "z", "yh", "c")
    return jax.shard_map(
        on_device,
        mesh=split,
        in_specs=(P(seq, "h"), P(seq, "h"), P(seq, "h"), P(seq, "h"), P("h", None), P(seq, None), P(seq)),
        out_specs=(P(seq, "h"), P(seq, "h"), P(seq, "h"), P(seq, "h"), P("h", None)),
        check_vma=False,
    )
```

```python
import math

import jax
import jax.numpy as jnp
from jax import lax
from jax.experimental import pallas as pl
from jax.experimental.pallas import tpu as pltpu
from jax.sharding import Mesh
from jax.sharding import PartitionSpec as P

F32, BF16 = jnp.float32, jnp.bfloat16
VM = pl.BlockSpec(memory_space=pltpu.VMEM)
SM = pl.BlockSpec(memory_space=pltpu.SMEM)
ANY = pl.BlockSpec(memory_space=pl.ANY)
NEG = -1e30
MIDG = 8
FARG = 128


def dot(a, b):
    return lax.dot_general(a, b, (((1,), (0,)), ((), ())), preferred_element_type=F32)


def dot_nt(a, b):
    return lax.dot_general(a, b, (((1,), (1,)), ((), ())), preferred_element_type=F32)


def fold(x, op):
    return op(x.reshape(x.shape[0] // 8, 8, x.shape[1]), axis=0)


def up(value):
    return value.astype(F32)


MESH = pl.DeviceIdType.MESH


class Place:
    def __init__(self):
        self.x, self.z = lax.axis_index("x"), lax.axis_index("z")
        self.yh, self.c, self.h = lax.axis_index("yh"), lax.axis_index("c"), lax.axis_index("h")
        self.plane = 8 * self.x + self.z
        self.shard = 2 * self.yh + self.c
        self.core = {"c": 1 - self.c}
        self.far = {"yh": 1 - self.yh}
        self.diagonal = {"yh": 1 - self.yh, "c": 1 - self.c}
        self.head = {"h": 1 - self.h}

    def along_z(self, i):
        return lax.rem(self.z + i, 8)

    def along_x(self, i):
        return lax.rem(self.x + i, 4)

    def next_plane(self, step):
        to = lax.rem(self.plane + step + 32, 32)
        return {"x": to // 8, "z": lax.rem(to, 8)}

    def next_shard(self, step):
        to = lax.rem(4 * self.plane + self.shard + step + 128, 128)
        return {"x": to // 32, "z": lax.rem(to // 4, 8), "yh": lax.rem(to // 2, 2), "c": lax.rem(to, 2)}

    def greet(self, diagonal):
        peers = [self.core, self.far, self.head, *[self.next_plane(d) for d in (1, 2, 3, -1, -2, -3)], self.next_shard(1), self.next_shard(-1)]
        peers += [{"z": self.along_z(i)} for i in range(1, 8)]
        peers += [{"x": self.along_x(i)} for i in range(1, 4)]
        peers += [{"x": self.along_x(i), "yh": 1 - self.yh} for i in range(1, 4)]
        if diagonal:
            peers.append(self.diagonal)
        barrier = pltpu.get_barrier_semaphore()
        for peer in peers:
            pl.semaphore_signal(barrier, inc=1, device_id=peer, device_id_type=MESH)
        return barrier, len(peers)


class Mail:
    def __init__(self, send_sems, recv_sems):
        self.sems, self.used, self.all = (send_sems, recv_sems), 0, []

    def send(self, source, target, device):
        at = self.used
        self.used += 1
        copy = pltpu.make_async_remote_copy(
            src_ref=source, dst_ref=target, send_sem=self.sems[0].at[at], recv_sem=self.sems[1].at[at],
            device_id=device, device_id_type=MESH)
        copy.start()
        self.all.append(copy)
        return copy

    def finish(self):
        for copy in self.all:
            copy.wait_send()


def layer_kernel(q_hbm, k_hbm, v_hbm, g_hbm, w_hbm, keep_ref, frame_ref,
                 out_hbm, dq_hbm, kg_hbm, vg_hbm, weight_hbm,
                 out_ref, dq_ref, kg_ref, vg_ref, weight_ref,
                 q, k, v, g, w, rim, go, wo, pooled, win, last, coarse, coarse4, mixed,
                 kaug, vcat, kt, vt, qaugT, gT, qm, gm, sbuf, dbuf, pbuf, tops, stats,
                 attT, att, atto, dqT, wg, wgb, wgr, wx, wxr, wz, wzr, wall,
                 near, rimg, rimr, wing, winr, acc, fars, farr, outs, backs, lines,
                 cg, cr, cx, cxr, cz, czr, cp, cpr, cfull,
                 load_sems, store_sems, send_sems, recv_sems):
    at = Place()
    c, x, z, yh, h, shard = at.c, at.x, at.z, at.yh, at.h, at.shard
    p = 4 * at.plane + shard
    loads = [pltpu.make_async_copy(a, b, load_sems.at[n])
             for n, (a, b) in enumerate(((k_hbm, k), (v_hbm, v), (g_hbm, g), (w_hbm, w), (q_hbm, q)))]
    for load in loads[:2]:
        load.start()
    barrier, count = at.greet(True)
    stores = []

    def store(n, source, target):
        copy = pltpu.make_async_copy(source, target, store_sems.at[n])
        copy.start()
        stores.append(copy)

    def lanes(n, size=256):
        return pl.ds(pl.multiple_of(size * n, size), size)

    row = lax.broadcasted_iota(jnp.int32, (80, 512), 0)
    token = lax.broadcasted_iota(jnp.int32, (80, 512), 1)
    owner = jnp.where(row < 64, row, 128 + (row - 64) - 4 * shard)
    group = jnp.where(row < 64, token // MIDG, 128 + token // FARG)
    ones = jnp.where(owner == group, 1.0, 0.0).astype(BF16)
    kind = lax.broadcasted_iota(jnp.int32, (80, 256), 0)
    me, peer = 2 * c + yh, 2 * c + 1 - yh
    loads[0].wait()
    keys = (dot(ones, k[...]) / jnp.where(kind < 64, math.sqrt(MIDG), math.sqrt(FARG))).astype(BF16)
    pooled[me, :, 0:256] = keys[0:64]
    coarse4[me, :, 0:256] = keys[64:80]
    loads[1].wait()
    values = (dot(ones, v[...]) / jnp.where(kind < 64, float(MIDG), float(FARG))).astype(BF16)
    pooled[me, :, 256:512] = values[0:64]
    coarse4[me, :, 256:512] = values[64:80]
    for load in loads[2:]:
        load.start()
    pl.semaphore_wait(barrier, count)

    mail = Mail(send_sems, recv_sems)
    ahead = at.next_plane(1)

    def relay(source, slot, place):
        target = last.at[place] if slot == 0 else win.at[slot, place]
        return mail.send(source, target, ahead)

    def share(slot, place):
        part = last.at[place] if slot == 0 else win.at[slot, place]
        return mail.send(part, part, at.core)

    over_plane = [mail.send(coarse4.at[me], coarse4.at[me], who) for who in (at.diagonal, at.far, at.core)]
    far = mail.send(pooled.at[me], pooled.at[me], at.far)
    hop_a1 = relay(pooled.at[me], 2, me)
    beside_a = mail.send(pooled.at[me], pooled.at[me], at.core)

    lane = lax.broadcasted_iota(jnp.int32, (16, 128), 1)

    def tile(bias0, bias1):
        return jnp.where(lane == 0, bias0, jnp.where(lane == 1, bias1, 0.0)).astype(BF16)

    def shut(seen):
        return jnp.where(seen, 0.0, NEG).astype(F32)

    def put(ci, at_row, value):
        for r in range(2):
            kaug[r, ci, at_row:at_row + value.shape[0], 128:256] = value

    first = tile(shut((frame_ref[0] == 1) & (p > 0)), jnp.float32(0.0))
    second = tile(jnp.float32(0.0), shut(frame_ref[1] == 1))
    for t in range(16):
        put(0, 16 * t, first)
        put(1, 16 * t, second)
    put(2, 0, jnp.zeros((256, 128), BF16))
    for slot in range(3):
        for n in range(4):
            j = 2 * (n % 2) + n // 2
            index = lax.rem(4 * slot + j - shard + 12, 12)
            real = p - 12 + index >= 0
            for r in range(4):
                keep0 = (keep_ref[0, 4 * index + r] == 1) & real
                keep1 = (keep_ref[1, 4 * index + r] == 1) & real
                if r >= 2:
                    keep0 = keep0 & (index < 11)
                put(3 + slot, 64 * n + 16 * r, tile(shut(keep0), shut(keep1)))
    rows = lax.broadcasted_iota(jnp.int32, (256, 128), 0)
    columns = lax.broadcasted_iota(jnp.int32, (256, 128), 1)
    for half in range(2):
        limit = 4 * p - 2 - 256 * half + 2 * columns
        put(6 + half, 0, jnp.where((columns < 2) & (rows >= limit), NEG, 0.0).astype(BF16))

    sub = lax.broadcasted_iota(jnp.int32, (128, 256), 0)
    subq = lax.broadcasted_iota(jnp.int32, (128, 512), 0)
    zero = jnp.zeros((), BF16)

    def by_head(source, b, r, transposed, plain):
        value = source[256 * b:256 * b + 256, 128 * r:128 * r + 128]
        turned = value.T
        for head in range(2):
            rest = slice(256 * head, 256 * head + 256)
            transposed[b, r, 0:128, rest] = jnp.where(sub // 64 == head, turned, zero)
            plain[b, r, rest, :] = jnp.where(columns // 64 == head, value, zero)

    loads[4].wait()
    q[...] = q[...] * jnp.asarray(0.125, BF16)
    for b in range(2):
        for r in range(2):
            by_head(q, b, r, qaugT, qm)
            qaugT[b, r, 128:256, :] = jnp.where(subq == b, 1.0, 0.0).astype(BF16)
            tops[b, r] = jnp.full((8, 512), NEG, F32)

    def prepare(ci):
        for r in range(2):
            lo, hi = slice(128 * r, 128 * r + 128), slice(256 + 128 * r, 384 + 128 * r)
            if ci == 0:
                kk, vv = rim[:, lo], rim[:, hi]
            elif ci < 3:
                kk, vv = k[256 * (ci - 1):256 * ci, lo], v[256 * (ci - 1):256 * ci, lo]
            elif ci < 6:
                kk, vv = win[ci - 3, :, :, lo].reshape(256, 128), win[ci - 3, :, :, hi].reshape(256, 128)
            else:
                part = slice(16 * (ci - 6), 16 * (ci - 5))
                kk, vv = coarse[part, :, lo].reshape(256, 128), coarse[part, :, hi].reshape(256, 128)
            kaug[r, ci, :, 0:128] = kk
            vcat[r, ci] = vv
            kt[r, ci] = kk.T
            vt[r, ci] = vv.T

    causal = lax.broadcasted_iota(jnp.int32, (256, 512), 0) <= lax.broadcasted_iota(jnp.int32, (256, 512), 1) % 256

    def uses(ci):
        for b in range(2):
            if ci > 2:
                yield b, ci - 1
            elif 0 <= ci - b < 2:
                yield b, ci - b

    def score(ci):
        prepare(ci)
        for r in range(2):
            for b, n in uses(ci):
                value = dot(kaug[r, ci], qaugT[b, r])
                if n == 1:
                    value = jnp.where(causal, value, NEG)
                sbuf[b, r, n] = value
                tops[b, r] = jnp.maximum(tops[b, r], fold(value, jnp.max))

    half = lanes(c)
    for copy in over_plane:
        copy.wait_recv()
    total = up(coarse4[0, :, half])
    for n in range(1, 4):
        total = total + up(coarse4[n, :, half])
    coarse[at.plane, :, half] = total.astype(BF16)
    mine = coarse.at[at.plane, :, half]
    over_z = [mail.send(mine, mine, {"z": at.along_z(i)}) for i in range(1, 8)]
    hop_a1.wait_recv()
    hop_a2 = relay(win.at[2, me], 1, me)
    share_a1 = share(2, me)
    far.wait_recv()
    hop_b1 = relay(pooled.at[peer], 2, peer)
    beside_b = mail.send(pooled.at[peer], pooled.at[peer], at.core)
    loads[2].wait()
    to_g = mail.send(g, go, at.head)
    to_k = mail.send(k.at[256:512, :], rim.at[:, 0:256], at.next_shard(1))
    to_v = mail.send(v.at[256:512, :], rim.at[:, 256:512], at.next_shard(1))
    score(1)
    hop_a2.wait_recv()
    hop_a3 = relay(win.at[1, me], 0, me)
    share_a2 = share(1, me)
    hop_b1.wait_recv()
    hop_b2 = relay(win.at[2, peer], 1, peer)
    share_b1 = share(2, peer)
    score(2)
    for copy in over_z:
        copy.wait_recv()
    line = coarse.at[pl.ds(8 * x, 8), :, half]
    over_x = [mail.send(line, line, {"x": at.along_x(i)}) for i in range(1, 4)]
    share_a1.wait_recv()
    share_b1.wait_recv()
    hop_a3.wait_recv()
    share_a3 = share(0, me)
    hop_b2.wait_recv()
    hop_b3 = relay(win.at[1, peer], 0, peer)
    share_b2 = share(1, peer)
    score(5)
    to_k.wait_recv()
    to_v.wait_recv()
    score(0)
    share_a2.wait_recv()
    share_b2.wait_recv()
    score(4)
    hop_b3.wait_recv()
    share_b3 = share(0, peer)
    for copy in over_x:
        copy.wait_recv()
    whole = coarse.at[:, :, half]
    share_coarse = mail.send(whole, whole, at.core)
    loads[3].wait()
    to_g.wait_recv()
    mixed[...] = (dot_nt(g[...], w[:, lanes(h)]) + dot_nt(go[...], w[:, lanes(1 - h)])).astype(BF16)
    for b in range(2):
        for r in range(2):
            by_head(mixed, b, r, gT, gm)
    share_a3.wait_recv()
    share_b3.wait_recv()
    beside_a.wait_recv()
    beside_b.wait_recv()
    for n in range(4):
        win[0, n] = jnp.where(2 * (n % 2) + n // 2 >= shard, last[n], pooled[n])
    score(3)
    share_coarse.wait_recv()
    score(6)
    score(7)

    for r in range(2):
        for b in range(2):
            top = jnp.max(tops[b, r], axis=0, keepdims=True)
            total = jnp.zeros((8, 512), F32)
            for n in range(7):
                e = jnp.exp(sbuf[b, r, n] - top)
                sbuf[b, r, n] = e
                total = total + fold(e, jnp.sum)
            inv = 1.0 / jnp.sum(total, axis=0, keepdims=True)
            stats[b, r, 0:1] = inv
            mix = [jnp.zeros((64, 256), F32)] * 2
            for n in range(7):
                ci = n + 1 if n >= 2 else n + b
                pr = (sbuf[b, r, n] * inv).astype(BF16)
                pbuf[b, r, n] = pr
                for head in range(2):
                    mix[head] = mix[head] + dot(vt[r, ci, 64 * head:64 * head + 64, :], pr[:, 256 * head:256 * head + 256])
            for head in range(2):
                attT[r, 64 * head:64 * head + 64, 256 * b:256 * b + 256] = mix[head].astype(BF16)
        att[:, 128 * r:128 * r + 128] = attT[r].T
    turned = attT[...].reshape(256, 512)
    wg[:, lanes(h)] = dot(turned, g[...]) * (1.0 / 256.0)
    wg[:, lanes(1 - h)] = dot(turned, go[...]) * (1.0 / 256.0)
    wgb[...] = wg[pl.ds(pl.multiple_of(128 * (1 - c), 128), 128), :].astype(BF16)
    to_w = mail.send(wgb, wgr, at.core)
    to_att = mail.send(att, atto, at.head)
    to_wo = mail.send(w.at[:, lanes(1 - h)], wo, at.head)
    for b in range(2):
        for r in range(2):
            dqT[b, r] = jnp.zeros((128, 256), F32)

    def grade(r):
        for b in range(2):
            centre = jnp.zeros((8, 512), F32)
            for n in range(7):
                ci = n + 1 if n >= 2 else n + b
                graded = dot(vcat[r, ci], gT[b, r])
                dbuf[b, r, n] = graded
                centre = centre + fold(sbuf[b, r, n] * graded, jnp.sum)
            stats[b, r, 1:2] = jnp.sum(centre, axis=0, keepdims=True) * stats[b, r, 0:1]

    def gradients(r, ci):
        dk, dv = None, None
        for b, n in uses(ci):
            inv, centre = stats[b, r, 0:1], stats[b, r, 1:2]
            ds = (sbuf[b, r, n] * inv * (dbuf[b, r, n] - centre)).astype(BF16)
            for head in range(2):
                some = slice(64 * head, 64 * head + 64)
                dqT[b, r, some, :] += dot(kt[r, ci, some, :], ds[:, 256 * head:256 * head + 256])
            one, two = dot(ds, qm[b, r]), dot(pbuf[b, r, n], gm[b, r])
            dk, dv = (one, two) if dk is None else (dk + one, dv + two)
        for cols, value in ((slice(0, 128), dk), (slice(128, 256), dv)):
            if ci == 0:
                rimg[r, :, cols] = value.astype(BF16)
            elif ci < 3:
                near[r, 256 * (ci - 1):256 * ci, cols] = value
            elif ci < 6:
                wing[r, ci - 3, :, :, cols] = value.astype(BF16).reshape(4, 64, 128)
            else:
                cg[r, 16 * (ci - 6):16 * (ci - 5), :, cols] = value.astype(BF16).reshape(16, 16, 128)

    def finish_queries(r):
        for b in range(2):
            dq_ref[256 * b:256 * b + 256, 128 * r:128 * r + 128] = (dqT[b, r] * 0.125).astype(BF16).T

    def send_window(r):
        return mail.send(wing.at[r, :, pl.ds(2 * (1 - c), 2)], winr.at[r], at.core)

    def to_far_plane(r):
        beside = 2 * yh + 1 - c
        for n in range(2):
            j = 2 * n + c
            own, got = up(wing[r, 0, 2 * c + n]), up(winr[r, 0, n])
            acc[r, n, 3] = jnp.where(j >= shard, own, 0.0) + jnp.where(j >= beside, got, 0.0)
            acc[r, n, 0] = jnp.where(j >= shard, 0.0, own) + jnp.where(j >= beside, 0.0, got)
            for m in range(2):
                acc[r, n, 2 - m] = up(wing[r, 1 + m, 2 * c + n]) + up(winr[r, 1 + m, n])
        fars[r] = acc[r, 1 - yh].astype(BF16)
        return mail.send(fars.at[r], farr.at[r], at.far)

    def to_owners(r):
        total = acc[r, yh] + up(farr[r])
        acc[r, yh] = total
        outs[r] = total[1:4].astype(BF16)
        return [mail.send(outs.at[r, d - 1], backs.at[r, d - 1], at.next_plane(-d)) for d in (3, 2, 1)]

    grade(0)
    to_w.wait_recv()
    wx[...] = (wg[pl.ds(pl.multiple_of(128 * c, 128), 128), :] + up(wgr[...])).astype(BF16).reshape(4, 32, 512)
    to_wx = [mail.send(wx.at[at.along_x(i)], wxr.at[i - 1], {"x": at.along_x(i)}) for i in range(1, 4)]
    gradients(0, 6)
    gradients(0, 7)
    grade(1)
    gradients(1, 6)
    gradients(1, 7)
    to_c = mail.send(cg.at[:, :, :, lanes(1 - c, 128)], cr, at.core)
    for copy in to_wx:
        copy.wait_recv()
    total = up(wx[x])
    for i in range(3):
        total = total + up(wxr[i])
    for n in range(8):
        wz[n] = total[16 * (n // 4):16 * (n // 4) + 16, 128 * (n % 4):128 * (n % 4) + 128]
    wzr[z, yh] = wz[z]
    to_wz = [mail.send(wz.at[at.along_z(i)], wzr.at[z, yh], {"z": at.along_z(i), "yh": yh if n == 0 else 1 - yh})
             for i in range(8) for n in range(2) if i + n > 0]
    gradients(0, 3)
    gradients(0, 4)
    to_c.wait_recv()
    cx[...] = (up(cg[:, :, :, lanes(c, 128)]) + up(cr[...])).astype(BF16)
    to_cx = [mail.send(cx.at[:, pl.ds(8 * at.along_x(i), 8)], cxr.at[i - 1], {"x": at.along_x(i)}) for i in range(1, 4)]
    gradients(0, 5)
    to_win0 = send_window(0)
    gradients(1, 3)
    gradients(1, 4)
    to_win0.wait_recv()
    to_far0 = to_far_plane(0)
    gradients(1, 5)
    to_win1 = send_window(1)
    for copy in to_wz:
        copy.wait_recv()
    total = wzr[0, 0]
    for n in range(1, 16):
        total = total + wzr[n // 2, n % 2]
    wall[z] = total
    to_wall = [mail.send(wall.at[z], wall.at[z], {"z": at.along_z(i)}) for i in range(1, 8)]
    gradients(0, 0)
    gradients(1, 0)
    to_rim0 = mail.send(rimg.at[0], rimr.at[0], at.next_shard(-1))
    to_rim1 = mail.send(rimg.at[1], rimr.at[1], at.next_shard(-1))
    to_win1.wait_recv()
    to_far1 = to_far_plane(1)
    for copy in to_cx:
        copy.wait_recv()
    total = up(cx[:, pl.ds(8 * x, 8)])
    for i in range(3):
        total = total + up(cxr[i])
    cz[...] = total.astype(BF16)
    to_cz = [mail.send(cz.at[:, at.along_z(i)], czr.at[i - 1], {"z": at.along_z(i)}) for i in range(1, 8)]
    gradients(0, 1)
    gradients(0, 2)
    finish_queries(0)
    to_far0.wait_recv()
    to_own0 = to_owners(0)
    gradients(1, 1)
    gradients(1, 2)
    finish_queries(1)
    store(0, dq_ref, dq_hbm)
    for copy in to_wall:
        copy.wait_recv()
    for n in range(8):
        lines[c, x, 16 * (n // 4):16 * (n // 4) + 16, 128 * (n % 4):128 * (n % 4) + 128] = wall[n].astype(BF16)
    line = lines.at[c, x]
    to_line = [mail.send(line, line, {"x": at.along_x(i)}) for i in range(1, 4)]
    to_far1.wait_recv()
    to_own1 = to_owners(1)
    to_att.wait_recv()
    to_wo.wait_recv()
    out_ref[...] = (dot(att[...], w[:, lanes(h)]) + dot(atto[...], wo[...])).astype(BF16)
    store(1, out_ref, out_hbm)
    for copy in to_cz:
        copy.wait_recv()
    total = up(cz[:, z])
    for i in range(7):
        total = total + up(czr[i])
    cp[...] = total.astype(BF16)
    to_cp = [mail.send(cp, cpr.at[n], who) for n, who in enumerate((at.far, at.core, at.diagonal))]
    for copy in to_line:
        copy.wait_recv()
    to_half = mail.send(lines.at[c], lines.at[c], at.core)
    for copy in to_cp:
        copy.wait_recv()
    for r in range(2):
        cfull[r, :, lanes(c, 128)] = up(cp[r]) + up(cpr[0, r])
        cfull[r, :, lanes(1 - c, 128)] = up(cpr[1, r]) + up(cpr[2, r])
    to_half.wait_recv()
    weight_ref[...] = up(lines[...])
    store(4, weight_ref, weight_hbm)
    token = lax.broadcasted_iota(jnp.int32, (512, 80), 0)
    row = lax.broadcasted_iota(jnp.int32, (512, 80), 1)
    spread = jnp.where(jnp.where(row < 64, token // MIDG, 64 + 4 * shard + token // FARG) == row, 1.0, 0.0).astype(BF16)
    row = lax.broadcasted_iota(jnp.int32, (80, 256), 0)
    value_lane = lax.broadcasted_iota(jnp.int32, (80, 256), 1) >= 128
    divisor = jnp.where(row < 64, jnp.where(value_lane, float(MIDG), math.sqrt(MIDG)), jnp.where(value_lane, float(FARG), math.sqrt(FARG)))
    for r, to_own, to_rim in ((0, to_own0, to_rim0), (1, to_own1, to_rim1)):
        to_rim.wait_recv()
        for copy in to_own:
            copy.wait_recv()
        middle = acc[r, yh, 0] + up(backs[r, 0]) + up(backs[r, 1]) + up(backs[r, 2])
        pools = jnp.concatenate([middle, cfull[r]], axis=0) / divisor
        high = pools.astype(BF16)
        low = (pools - up(high)).astype(BF16)
        added = dot(spread, high) + dot(spread, low) + near[r]
        for target, cols in ((kg_ref, slice(0, 128)), (vg_ref, slice(128, 256))):
            target[0:256, 128 * r:128 * r + 128] = added[0:256, cols].astype(BF16)
            target[256:512, 128 * r:128 * r + 128] = (added[256:512, cols] + up(rimr[r, :, cols])).astype(BF16)
    store(2, kg_ref, kg_hbm)
    store(3, vg_ref, vg_hbm)
    for copy in stores:
        copy.wait()
    mail.finish()


def handed_on(*refs):
    for n in range(5):
        refs[5 + n][...] = refs[n][...]


def on_device(queries, key_vectors, value_vectors, out_grad, out_weight, mid_keep, frame_keep):
    B, S = (lambda *s: pltpu.VMEM(s, BF16)), (lambda *s: pltpu.VMEM(s, F32))
    T = jax.ShapeDtypeStruct((512, 256), BF16)
    output, dq, kg, vg, weight = pl.pallas_call(
        layer_kernel,
        out_shape=[T, T, T, T, jax.ShapeDtypeStruct((2, 4, 32, 512), F32)],
        in_specs=[ANY] * 5 + [SM] * 2,
        out_specs=[ANY] * 5,
        scratch_shapes=[
            B(512, 256), B(512, 256), B(512, 256), B(512, 256), S(2, 4, 32, 512),
            B(512, 256), B(512, 256), B(512, 256), B(512, 256), B(256, 512), B(256, 512), B(512, 256), B(256, 256),
            B(4, 64, 512), B(3, 4, 64, 512), B(4, 64, 512), B(32, 16, 512), B(4, 16, 512), B(512, 256),
            B(2, 8, 256, 256), B(2, 8, 256, 128), B(2, 8, 128, 256), B(2, 8, 128, 256),
            B(2, 2, 256, 512), B(2, 2, 128, 512), B(2, 2, 512, 128), B(2, 2, 512, 128),
            S(2, 2, 7, 256, 512), S(2, 2, 7, 256, 512), B(2, 2, 7, 256, 512), S(2, 2, 8, 512), S(2, 2, 8, 512),
            B(2, 128, 512), B(512, 256), B(512, 256), S(2, 2, 128, 256), S(256, 512), B(128, 512), B(128, 512),
            B(4, 32, 512), B(3, 32, 512), S(8, 16, 128), S(8, 2, 16, 128), S(8, 16, 128),
            S(2, 512, 256), B(2, 256, 256), B(2, 256, 256), B(2, 3, 4, 64, 256), B(2, 3, 2, 64, 256),
            S(2, 2, 4, 64, 256), B(2, 4, 64, 256), B(2, 4, 64, 256), B(2, 3, 64, 256), B(2, 3, 64, 256), B(2, 4, 32, 512),
            B(2, 32, 16, 256), B(2, 32, 16, 128), B(2, 32, 16, 128), B(3, 2, 8, 16, 128), B(2, 8, 16, 128),
            B(7, 2, 16, 128), B(2, 16, 128), B(3, 2, 16, 128), S(2, 16, 256),
            pltpu.SemaphoreType.DMA((5,)), pltpu.SemaphoreType.DMA((5,)), pltpu.SemaphoreType.DMA((90,)), pltpu.SemaphoreType.DMA((90,))],
        compiler_params=pltpu.CompilerParams(collective_id=0, has_side_effects=True, vmem_limit_bytes=60 * 2**20),
        name="layer",
    )(queries, key_vectors, value_vectors, out_grad, out_weight, mid_keep, frame_keep)
    shapes = [T, T, T, T, jax.ShapeDtypeStruct((2, 4, 32, 512), F32)]
    output, dq, kg, vg, weight = pl.pallas_call(
        handed_on,
        out_shape=shapes,
        in_specs=[VM] * 5,
        out_specs=[VM] * 5,
        name="handed_on",
    )(output, dq, kg, vg, weight)
    return output, dq, kg, vg, weight.reshape(256, 512)


def solution(mesh):
    split = Mesh(mesh.devices.reshape(4, 8, 2, 2, 2), ("x", "z", "yh", "c", "h"))
    seq = ("x", "z", "yh", "c")
    return jax.shard_map(
        on_device,
        mesh=split,
        in_specs=(P(seq, "h"), P(seq, "h"), P(seq, "h"), P(seq, "h"), P("h", None), P(seq, None), P(seq)),
        out_specs=(P(seq, "h"), P(seq, "h"), P(seq, "h"), P(seq, "h"), P("h", None)),
        check_vma=False,
    )
```

```python
import math

import jax
import jax.numpy as jnp
from jax import lax
from jax.experimental import pallas as pl
from jax.experimental.pallas import tpu as pltpu
from jax.sharding import Mesh
from jax.sharding import PartitionSpec as P

F32, BF16 = jnp.float32, jnp.bfloat16
VM = pl.BlockSpec(memory_space=pltpu.VMEM)
SM = pl.BlockSpec(memory_space=pltpu.SMEM)
ANY = pl.BlockSpec(memory_space=pl.ANY)
NEG = -1e30
MIDG = 8
FARG = 128


def dot(a, b):
    return lax.dot_general(a, b, (((1,), (0,)), ((), ())), preferred_element_type=F32)


def dot_nt(a, b):
    return lax.dot_general(a, b, (((1,), (1,)), ((), ())), preferred_element_type=F32)


def fold(x, op):
    return op(x.reshape(x.shape[0] // 8, 8, x.shape[1]), axis=0)


def up(value):
    return value.astype(F32)


MESH = pl.DeviceIdType.MESH


class Place:
    def __init__(self):
        self.x, self.z = lax.axis_index("x"), lax.axis_index("z")
        self.yh, self.c, self.h = lax.axis_index("yh"), lax.axis_index("c"), lax.axis_index("h")
        self.plane = 8 * self.x + self.z
        self.shard = 2 * self.yh + self.c
        self.core = {"c": 1 - self.c}
        self.far = {"yh": 1 - self.yh}
        self.diagonal = {"yh": 1 - self.yh, "c": 1 - self.c}
        self.head = {"h": 1 - self.h}

    def along_z(self, i):
        return lax.rem(self.z + i, 8)

    def along_x(self, i):
        return lax.rem(self.x + i, 4)

    def next_plane(self, step):
        to = lax.rem(self.plane + step + 32, 32)
        return {"x": to // 8, "z": lax.rem(to, 8)}

    def next_shard(self, step):
        to = lax.rem(4 * self.plane + self.shard + step + 128, 128)
        return {"x": to // 32, "z": lax.rem(to // 4, 8), "yh": lax.rem(to // 2, 2), "c": lax.rem(to, 2)}

    def greet(self, diagonal):
        peers = [self.core, self.far, self.head, *[self.next_plane(d) for d in (1, 2, 3, -1, -2, -3)], self.next_shard(1), self.next_shard(-1)]
        peers += [{"z": self.along_z(i)} for i in range(1, 8)]
        peers += [{"x": self.along_x(i)} for i in range(1, 4)]
        if diagonal:
            peers.append(self.diagonal)
        barrier = pltpu.get_barrier_semaphore()
        for peer in peers:
            pl.semaphore_signal(barrier, inc=1, device_id=peer, device_id_type=MESH)
        return barrier, len(peers)


class Mail:
    def __init__(self, send_sems, recv_sems):
        self.sems, self.used, self.all = (send_sems, recv_sems), 0, []

    def send(self, source, target, device):
        at = self.used
        self.used += 1
        copy = pltpu.make_async_remote_copy(
            src_ref=source, dst_ref=target, send_sem=self.sems[0].at[at], recv_sem=self.sems[1].at[at],
            device_id=device, device_id_type=MESH)
        copy.start()
        self.all.append(copy)
        return copy

    def finish(self):
        for copy in self.all:
            copy.wait_send()


def layer_kernel(q_hbm, k_hbm, v_hbm, g_hbm, w_hbm, keep_ref, frame_ref,
                 out_hbm, dq_hbm, kg_hbm, vg_hbm, weight_hbm,
                 out_ref, dq_ref, kg_ref, vg_ref,
                 q, k, v, g, w, rim, go, wo, pooled, win, last, coarse, coarse4, mixed,
                 kaug, vcat, kt, vt, qaugT, gT, qm, gm, sbuf, dbuf, pbuf, tops, stats,
                 attT, att, atto, dqT, wg, wgb, wgr, wx, wxr, wz, wzr, wall,
                 near, rimg, rimr, wing, winr, acc, fars, farr, outs, backs, lines,
                 cg, cr, cx, cxr, cz, czr, cp, cpr, cfull,
                 load_sems, store_sems, send_sems, recv_sems):
    at = Place()
    c, x, z, yh, h, shard = at.c, at.x, at.z, at.yh, at.h, at.shard
    p = 4 * at.plane + shard
    loads = [pltpu.make_async_copy(a, b, load_sems.at[n])
             for n, (a, b) in enumerate(((k_hbm, k), (v_hbm, v), (g_hbm, g), (w_hbm, w), (q_hbm, q)))]
    for load in loads[:2]:
        load.start()
    barrier, count = at.greet(True)
    stores = []

    def store(n, source, target):
        copy = pltpu.make_async_copy(source, target, store_sems.at[n])
        copy.start()
        stores.append(copy)

    def lanes(n, size=256):
        return pl.ds(pl.multiple_of(size * n, size), size)

    row = lax.broadcasted_iota(jnp.int32, (80, 512), 0)
    token = lax.broadcasted_iota(jnp.int32, (80, 512), 1)
    owner = jnp.where(row < 64, row, 128 + (row - 64) - 4 * shard)
    group = jnp.where(row < 64, token // MIDG, 128 + token // FARG)
    ones = jnp.where(owner == group, 1.0, 0.0).astype(BF16)
    kind = lax.broadcasted_iota(jnp.int32, (80, 256), 0)
    me, peer = 2 * c + yh, 2 * c + 1 - yh
    loads[0].wait()
    keys = (dot(ones, k[...]) / jnp.where(kind < 64, math.sqrt(MIDG), math.sqrt(FARG))).astype(BF16)
    pooled[me, :, 0:256] = keys[0:64]
    coarse4[me, :, 0:256] = keys[64:80]
    loads[1].wait()
    values = (dot(ones, v[...]) / jnp.where(kind < 64, float(MIDG), float(FARG))).astype(BF16)
    pooled[me, :, 256:512] = values[0:64]
    coarse4[me, :, 256:512] = values[64:80]
    for load in loads[2:]:
        load.start()
    pl.semaphore_wait(barrier, count)

    mail = Mail(send_sems, recv_sems)
    ahead = at.next_plane(1)

    def relay(source, slot, place):
        target = last.at[place] if slot == 0 else win.at[slot, place]
        return mail.send(source, target, ahead)

    def share(slot, place):
        part = last.at[place] if slot == 0 else win.at[slot, place]
        return mail.send(part, part, at.core)

    over_plane = [mail.send(coarse4.at[me], coarse4.at[me], who) for who in (at.diagonal, at.far, at.core)]
    far = mail.send(pooled.at[me], pooled.at[me], at.far)
    hop_a1 = relay(pooled.at[me], 2, me)
    beside_a = mail.send(pooled.at[me], pooled.at[me], at.core)

    lane = lax.broadcasted_iota(jnp.int32, (16, 128), 1)

    def tile(bias0, bias1):
        return jnp.where(lane == 0, bias0, jnp.where(lane == 1, bias1, 0.0)).astype(BF16)

    def shut(seen):
        return jnp.where(seen, 0.0, NEG).astype(F32)

    def put(ci, at_row, value):
        for r in range(2):
            kaug[r, ci, at_row:at_row + value.shape[0], 128:256] = value

    first = tile(shut((frame_ref[0] == 1) & (p > 0)), jnp.float32(0.0))
    second = tile(jnp.float32(0.0), shut(frame_ref[1] == 1))
    for t in range(16):
        put(0, 16 * t, first)
        put(1, 16 * t, second)
    put(2, 0, jnp.zeros((256, 128), BF16))
    for slot in range(3):
        for n in range(4):
            j = 2 * (n % 2) + n // 2
            index = lax.rem(4 * slot + j - shard + 12, 12)
            real = p - 12 + index >= 0
            for r in range(4):
                keep0 = (keep_ref[0, 4 * index + r] == 1) & real
                keep1 = (keep_ref[1, 4 * index + r] == 1) & real
                if r >= 2:
                    keep0 = keep0 & (index < 11)
                put(3 + slot, 64 * n + 16 * r, tile(shut(keep0), shut(keep1)))
    rows = lax.broadcasted_iota(jnp.int32, (256, 128), 0)
    columns = lax.broadcasted_iota(jnp.int32, (256, 128), 1)
    for half in range(2):
        limit = 4 * p - 2 - 256 * half + 2 * columns
        put(6 + half, 0, jnp.where((columns < 2) & (rows >= limit), NEG, 0.0).astype(BF16))

    sub = lax.broadcasted_iota(jnp.int32, (128, 256), 0)
    subq = lax.broadcasted_iota(jnp.int32, (128, 512), 0)
    zero = jnp.zeros((), BF16)

    def by_head(source, b, r, transposed, plain):
        value = source[256 * b:256 * b + 256, 128 * r:128 * r + 128]
        turned = value.T
        for head in range(2):
            rest = slice(256 * head, 256 * head + 256)
            transposed[b, r, 0:128, rest] = jnp.where(sub // 64 == head, turned, zero)
            plain[b, r, rest, :] = jnp.where(columns // 64 == head, value, zero)

    loads[4].wait()
    q[...] = q[...] * jnp.asarray(0.125, BF16)
    for b in range(2):
        for r in range(2):
            by_head(q, b, r, qaugT, qm)
            qaugT[b, r, 128:256, :] = jnp.where(subq == b, 1.0, 0.0).astype(BF16)
            tops[b, r] = jnp.full((8, 512), NEG, F32)

    def prepare(ci):
        for r in range(2):
            lo, hi = slice(128 * r, 128 * r + 128), slice(256 + 128 * r, 384 + 128 * r)
            if ci == 0:
                kk, vv = rim[:, lo], rim[:, hi]
            elif ci < 3:
                kk, vv = k[256 * (ci - 1):256 * ci, lo], v[256 * (ci - 1):256 * ci, lo]
            elif ci < 6:
                kk, vv = win[ci - 3, :, :, lo].reshape(256, 128), win[ci - 3, :, :, hi].reshape(256, 128)
            else:
                part = slice(16 * (ci - 6), 16 * (ci - 5))
                kk, vv = coarse[part, :, lo].reshape(256, 128), coarse[part, :, hi].reshape(256, 128)
            kaug[r, ci, :, 0:128] = kk
            vcat[r, ci] = vv
            kt[r, ci] = kk.T
            vt[r, ci] = vv.T

    causal = lax.broadcasted_iota(jnp.int32, (256, 512), 0) <= lax.broadcasted_iota(jnp.int32, (256, 512), 1) % 256

    def uses(ci):
        for b in range(2):
            if ci > 2:
                yield b, ci - 1
            elif 0 <= ci - b < 2:
                yield b, ci - b

    def score(ci):
        prepare(ci)
        for r in range(2):
            for b, n in uses(ci):
                value = dot(kaug[r, ci], qaugT[b, r])
                if n == 1:
                    value = jnp.where(causal, value, NEG)
                sbuf[b, r, n] = value
                tops[b, r] = jnp.maximum(tops[b, r], fold(value, jnp.max))

    half = lanes(c)
    for copy in over_plane:
        copy.wait_recv()
    total = up(coarse4[0, :, half])
    for n in range(1, 4):
        total = total + up(coarse4[n, :, half])
    coarse[at.plane, :, half] = total.astype(BF16)
    mine = coarse.at[at.plane, :, half]
    over_z = [mail.send(mine, mine, {"z": at.along_z(i)}) for i in range(1, 8)]
    hop_a1.wait_recv()
    hop_a2 = relay(win.at[2, me], 1, me)
    share_a1 = share(2, me)
    far.wait_recv()
    hop_b1 = relay(pooled.at[peer], 2, peer)
    beside_b = mail.send(pooled.at[peer], pooled.at[peer], at.core)
    loads[2].wait()
    to_g = mail.send(g, go, at.head)
    to_k = mail.send(k.at[256:512, :], rim.at[:, 0:256], at.next_shard(1))
    to_v = mail.send(v.at[256:512, :], rim.at[:, 256:512], at.next_shard(1))
    score(1)
    hop_a2.wait_recv()
    hop_a3 = relay(win.at[1, me], 0, me)
    share_a2 = share(1, me)
    hop_b1.wait_recv()
    hop_b2 = relay(win.at[2, peer], 1, peer)
    share_b1 = share(2, peer)
    score(2)
    for copy in over_z:
        copy.wait_recv()
    line = coarse.at[pl.ds(8 * x, 8), :, half]
    over_x = [mail.send(line, line, {"x": at.along_x(i)}) for i in range(1, 4)]
    share_a1.wait_recv()
    share_b1.wait_recv()
    hop_a3.wait_recv()
    share_a3 = share(0, me)
    hop_b2.wait_recv()
    hop_b3 = relay(win.at[1, peer], 0, peer)
    share_b2 = share(1, peer)
    score(5)
    to_k.wait_recv()
    to_v.wait_recv()
    score(0)
    share_a2.wait_recv()
    share_b2.wait_recv()
    score(4)
    hop_b3.wait_recv()
    share_b3 = share(0, peer)
    for copy in over_x:
        copy.wait_recv()
    whole = coarse.at[:, :, half]
    share_coarse = mail.send(whole, whole, at.core)
    loads[3].wait()
    to_g.wait_recv()
    mixed[...] = (dot_nt(g[...], w[:, lanes(h)]) + dot_nt(go[...], w[:, lanes(1 - h)])).astype(BF16)
    for b in range(2):
        for r in range(2):
            by_head(mixed, b, r, gT, gm)
    share_a3.wait_recv()
    share_b3.wait_recv()
    beside_a.wait_recv()
    beside_b.wait_recv()
    for n in range(4):
        win[0, n] = jnp.where(2 * (n % 2) + n // 2 >= shard, last[n], pooled[n])
    score(3)
    share_coarse.wait_recv()
    score(6)
    score(7)

    for r in range(2):
        for b in range(2):
            top = jnp.max(tops[b, r], axis=0, keepdims=True)
            total = jnp.zeros((8, 512), F32)
            for n in range(7):
                e = jnp.exp(sbuf[b, r, n] - top)
                sbuf[b, r, n] = e
                total = total + fold(e, jnp.sum)
            inv = 1.0 / jnp.sum(total, axis=0, keepdims=True)
            stats[b, r, 0:1] = inv
            mix = [jnp.zeros((64, 256), F32)] * 2
            for n in range(7):
                ci = n + 1 if n >= 2 else n + b
                pr = (sbuf[b, r, n] * inv).astype(BF16)
                pbuf[b, r, n] = pr
                for head in range(2):
                    mix[head] = mix[head] + dot(vt[r, ci, 64 * head:64 * head + 64, :], pr[:, 256 * head:256 * head + 256])
            for head in range(2):
                attT[r, 64 * head:64 * head + 64, 256 * b:256 * b + 256] = mix[head].astype(BF16)
        att[:, 128 * r:128 * r + 128] = attT[r].T
    turned = attT[...].reshape(256, 512)
    wg[:, lanes(h)] = dot(turned, g[...]) * (1.0 / 256.0)
    wg[:, lanes(1 - h)] = dot(turned, go[...]) * (1.0 / 256.0)
    wgb[...] = wg[pl.ds(pl.multiple_of(128 * (1 - c), 128), 128), :].astype(BF16)
    to_w = mail.send(wgb, wgr, at.core)
    to_att = mail.send(att, atto, at.head)
    to_wo = mail.send(w.at[:, lanes(1 - h)], wo, at.head)
    for b in range(2):
        for r in range(2):
            dqT[b, r] = jnp.zeros((128, 256), F32)

    def grade(r):
        for b in range(2):
            centre = jnp.zeros((8, 512), F32)
            for n in range(7):
                ci = n + 1 if n >= 2 else n + b
                graded = dot(vcat[r, ci], gT[b, r])
                dbuf[b, r, n] = graded
                centre = centre + fold(sbuf[b, r, n] * graded, jnp.sum)
            stats[b, r, 1:2] = jnp.sum(centre, axis=0, keepdims=True) * stats[b, r, 0:1]

    def gradients(r, ci):
        dk, dv = None, None
        for b, n in uses(ci):
            inv, centre = stats[b, r, 0:1], stats[b, r, 1:2]
            ds = (sbuf[b, r, n] * inv * (dbuf[b, r, n] - centre)).astype(BF16)
            for head in range(2):
                some = slice(64 * head, 64 * head + 64)
                dqT[b, r, some, :] += dot(kt[r, ci, some, :], ds[:, 256 * head:256 * head + 256])
            one, two = dot(ds, qm[b, r]), dot(pbuf[b, r, n], gm[b, r])
            dk, dv = (one, two) if dk is None else (dk + one, dv + two)
        for cols, value in ((slice(0, 128), dk), (slice(128, 256), dv)):
            if ci == 0:
                rimg[r, :, cols] = value.astype(BF16)
            elif ci < 3:
                near[r, 256 * (ci - 1):256 * ci, cols] = value
            elif ci < 6:
                wing[r, ci - 3, :, :, cols] = value.astype(BF16).reshape(4, 64, 128)
            else:
                cg[r, 16 * (ci - 6):16 * (ci - 5), :, cols] = value.astype(BF16).reshape(16, 16, 128)

    def finish_queries(r):
        for b in range(2):
            dq_ref[256 * b:256 * b + 256, 128 * r:128 * r + 128] = (dqT[b, r] * 0.125).astype(BF16).T

    def send_window(r):
        return mail.send(wing.at[r, :, pl.ds(2 * (1 - c), 2)], winr.at[r], at.core)

    def to_far_plane(r):
        beside = 2 * yh + 1 - c
        for n in range(2):
            j = 2 * n + c
            own, got = up(wing[r, 0, 2 * c + n]), up(winr[r, 0, n])
            acc[r, n, 3] = jnp.where(j >= shard, own, 0.0) + jnp.where(j >= beside, got, 0.0)
            acc[r, n, 0] = jnp.where(j >= shard, 0.0, own) + jnp.where(j >= beside, 0.0, got)
            for m in range(2):
                acc[r, n, 2 - m] = up(wing[r, 1 + m, 2 * c + n]) + up(winr[r, 1 + m, n])
        fars[r] = acc[r, 1 - yh].astype(BF16)
        return mail.send(fars.at[r], farr.at[r], at.far)

    def to_owners(r):
        total = acc[r, yh] + up(farr[r])
        acc[r, yh] = total
        outs[r] = total[1:4].astype(BF16)
        return [mail.send(outs.at[r, d - 1], backs.at[r, d - 1], at.next_plane(-d)) for d in (3, 2, 1)]

    grade(0)
    to_w.wait_recv()
    wx[...] = (wg[pl.ds(pl.multiple_of(128 * c, 128), 128), :] + up(wgr[...])).astype(BF16).reshape(4, 32, 512)
    to_wx = [mail.send(wx.at[at.along_x(i)], wxr.at[i - 1], {"x": at.along_x(i)}) for i in range(1, 4)]
    gradients(0, 6)
    gradients(0, 7)
    grade(1)
    gradients(1, 6)
    gradients(1, 7)
    to_c = mail.send(cg.at[:, :, :, lanes(1 - c, 128)], cr, at.core)
    for copy in to_wx:
        copy.wait_recv()
    total = up(wx[x])
    for i in range(3):
        total = total + up(wxr[i])
    for n in range(8):
        wz[n] = total[16 * (n // 4):16 * (n // 4) + 16, 128 * (n % 4):128 * (n % 4) + 128]
    wzr[z, yh] = wz[z]
    to_wz = [mail.send(wz.at[at.along_z(i)], wzr.at[z, yh], {"z": at.along_z(i), "yh": yh if n == 0 else 1 - yh})
             for i in range(8) for n in range(2) if i + n > 0]
    gradients(0, 3)
    gradients(0, 4)
    to_c.wait_recv()
    cx[...] = (up(cg[:, :, :, lanes(c, 128)]) + up(cr[...])).astype(BF16)
    to_cx = [mail.send(cx.at[:, pl.ds(8 * at.along_x(i), 8)], cxr.at[i - 1], {"x": at.along_x(i)}) for i in range(1, 4)]
    gradients(0, 5)
    to_win0 = send_window(0)
    gradients(1, 3)
    gradients(1, 4)
    to_win0.wait_recv()
    to_far0 = to_far_plane(0)
    gradients(1, 5)
    to_win1 = send_window(1)
    for copy in to_wz:
        copy.wait_recv()
    total = wzr[0, 0]
    for n in range(1, 16):
        total = total + wzr[n // 2, n % 2]
    wall[z] = total
    to_wall = [mail.send(wall.at[z], wall.at[z], {"z": at.along_z(i)}) for i in range(1, 8)]
    gradients(0, 0)
    gradients(1, 0)
    to_rim0 = mail.send(rimg.at[0], rimr.at[0], at.next_shard(-1))
    to_rim1 = mail.send(rimg.at[1], rimr.at[1], at.next_shard(-1))
    to_win1.wait_recv()
    to_far1 = to_far_plane(1)
    for copy in to_cx:
        copy.wait_recv()
    total = up(cx[:, pl.ds(8 * x, 8)])
    for i in range(3):
        total = total + up(cxr[i])
    cz[...] = total.astype(BF16)
    to_cz = [mail.send(cz.at[:, at.along_z(i)], czr.at[i - 1], {"z": at.along_z(i)}) for i in range(1, 8)]
    gradients(0, 1)
    gradients(0, 2)
    finish_queries(0)
    to_far0.wait_recv()
    to_own0 = to_owners(0)
    gradients(1, 1)
    gradients(1, 2)
    finish_queries(1)
    store(0, dq_ref, dq_hbm)
    for copy in to_wall:
        copy.wait_recv()
    for n in range(8):
        lines[c, x, 16 * (n // 4):16 * (n // 4) + 16, 128 * (n % 4):128 * (n % 4) + 128] = wall[n].astype(BF16)
    line = lines.at[c, x]
    to_line = [mail.send(line, line, {"x": at.along_x(i)}) for i in range(1, 4)]
    to_far1.wait_recv()
    to_own1 = to_owners(1)
    for copy in to_cz:
        copy.wait_recv()
    total = up(cz[:, z])
    for i in range(7):
        total = total + up(czr[i])
    cp[...] = total.astype(BF16)
    to_cp = [mail.send(cp, cpr.at[n], who) for n, who in enumerate((at.far, at.core, at.diagonal))]
    to_att.wait_recv()
    to_wo.wait_recv()
    out_ref[...] = (dot(att[...], w[:, lanes(h)]) + dot(atto[...], wo[...])).astype(BF16)
    store(1, out_ref, out_hbm)
    for copy in to_line:
        copy.wait_recv()
    to_half = mail.send(lines.at[c], lines.at[c], at.core)
    for copy in to_cp:
        copy.wait_recv()
    for r in range(2):
        cfull[r, :, lanes(c, 128)] = up(cp[r]) + up(cpr[0, r])
        cfull[r, :, lanes(1 - c, 128)] = up(cpr[1, r]) + up(cpr[2, r])
    to_half.wait_recv()
    store(4, lines, weight_hbm)
    token = lax.broadcasted_iota(jnp.int32, (512, 80), 0)
    row = lax.broadcasted_iota(jnp.int32, (512, 80), 1)
    spread = jnp.where(jnp.where(row < 64, token // MIDG, 64 + 4 * shard + token // FARG) == row, 1.0, 0.0).astype(BF16)
    row = lax.broadcasted_iota(jnp.int32, (80, 256), 0)
    value_lane = lax.broadcasted_iota(jnp.int32, (80, 256), 1) >= 128
    divisor = jnp.where(row < 64, jnp.where(value_lane, float(MIDG), math.sqrt(MIDG)), jnp.where(value_lane, float(FARG), math.sqrt(FARG)))
    for r, to_own, to_rim in ((0, to_own0, to_rim0), (1, to_own1, to_rim1)):
        to_rim.wait_recv()
        for copy in to_own:
            copy.wait_recv()
        middle = acc[r, yh, 0] + up(backs[r, 0]) + up(backs[r, 1]) + up(backs[r, 2])
        pools = jnp.concatenate([middle, cfull[r]], axis=0) / divisor
        high = pools.astype(BF16)
        low = (pools - up(high)).astype(BF16)
        added = dot(spread, high) + dot(spread, low) + near[r]
        for target, cols in ((kg_ref, slice(0, 128)), (vg_ref, slice(128, 256))):
            target[0:256, 128 * r:128 * r + 128] = added[0:256, cols].astype(BF16)
            target[256:512, 128 * r:128 * r + 128] = (added[256:512, cols] + up(rimr[r, :, cols])).astype(BF16)
    store(2, kg_ref, kg_hbm)
    store(3, vg_ref, vg_hbm)
    for copy in stores:
        copy.wait()
    mail.finish()


def handed_on(*refs):
    for n in range(4):
        refs[5 + n][...] = refs[n][...]
    refs[9][...] = up(refs[4][...])


def on_device(queries, key_vectors, value_vectors, out_grad, out_weight, mid_keep, frame_keep):
    B, S = (lambda *s: pltpu.VMEM(s, BF16)), (lambda *s: pltpu.VMEM(s, F32))
    T = jax.ShapeDtypeStruct((512, 256), BF16)
    output, dq, kg, vg, weight = pl.pallas_call(
        layer_kernel,
        out_shape=[T, T, T, T, jax.ShapeDtypeStruct((2, 4, 32, 512), BF16)],
        in_specs=[ANY] * 5 + [SM] * 2,
        out_specs=[ANY] * 5,
        scratch_shapes=[
            B(512, 256), B(512, 256), B(512, 256), B(512, 256),
            B(512, 256), B(512, 256), B(512, 256), B(512, 256), B(256, 512), B(256, 512), B(512, 256), B(256, 256),
            B(4, 64, 512), B(3, 4, 64, 512), B(4, 64, 512), B(32, 16, 512), B(4, 16, 512), B(512, 256),
            B(2, 8, 256, 256), B(2, 8, 256, 128), B(2, 8, 128, 256), B(2, 8, 128, 256),
            B(2, 2, 256, 512), B(2, 2, 128, 512), B(2, 2, 512, 128), B(2, 2, 512, 128),
            S(2, 2, 7, 256, 512), S(2, 2, 7, 256, 512), B(2, 2, 7, 256, 512), S(2, 2, 8, 512), S(2, 2, 8, 512),
            B(2, 128, 512), B(512, 256), B(512, 256), S(2, 2, 128, 256), S(256, 512), B(128, 512), B(128, 512),
            B(4, 32, 512), B(3, 32, 512), S(8, 16, 128), S(8, 2, 16, 128), S(8, 16, 128),
            S(2, 512, 256), B(2, 256, 256), B(2, 256, 256), B(2, 3, 4, 64, 256), B(2, 3, 2, 64, 256),
            S(2, 2, 4, 64, 256), B(2, 4, 64, 256), B(2, 4, 64, 256), B(2, 3, 64, 256), B(2, 3, 64, 256), B(2, 4, 32, 512),
            B(2, 32, 16, 256), B(2, 32, 16, 128), B(2, 32, 16, 128), B(3, 2, 8, 16, 128), B(2, 8, 16, 128),
            B(7, 2, 16, 128), B(2, 16, 128), B(3, 2, 16, 128), S(2, 16, 256),
            pltpu.SemaphoreType.DMA((5,)), pltpu.SemaphoreType.DMA((5,)), pltpu.SemaphoreType.DMA((90,)), pltpu.SemaphoreType.DMA((90,))],
        compiler_params=pltpu.CompilerParams(collective_id=0, has_side_effects=True, vmem_limit_bytes=60 * 2**20),
        name="layer",
    )(queries, key_vectors, value_vectors, out_grad, out_weight, mid_keep, frame_keep)
    shapes = [T, T, T, T, jax.ShapeDtypeStruct((2, 4, 32, 512), F32)]
    output, dq, kg, vg, weight = pl.pallas_call(
        handed_on,
        out_shape=shapes,
        in_specs=[VM] * 5,
        out_specs=[VM] * 5,
        name="handed_on",
    )(output, dq, kg, vg, weight)
    return output, dq, kg, vg, weight.reshape(256, 512)


def solution(mesh):
    split = Mesh(mesh.devices.reshape(4, 8, 2, 2, 2), ("x", "z", "yh", "c", "h"))
    seq = ("x", "z", "yh", "c")
    return jax.shard_map(
        on_device,
        mesh=split,
        in_specs=(P(seq, "h"), P(seq, "h"), P(seq, "h"), P(seq, "h"), P("h", None), P(seq, None), P(seq)),
        out_specs=(P(seq, "h"), P(seq, "h"), P(seq, "h"), P(seq, "h"), P("h", None)),
        check_vma=False,
    )
```

```python
import math

import jax
import jax.numpy as jnp
from jax import lax
from jax.experimental import pallas as pl
from jax.experimental.pallas import tpu as pltpu
from jax.sharding import Mesh
from jax.sharding import PartitionSpec as P

F32, BF16 = jnp.float32, jnp.bfloat16
VM = pl.BlockSpec(memory_space=pltpu.VMEM)
SM = pl.BlockSpec(memory_space=pltpu.SMEM)
ANY = pl.BlockSpec(memory_space=pl.ANY)
NEG = -1e30
MIDG = 8
FARG = 128


def dot(a, b):
    return lax.dot_general(a, b, (((1,), (0,)), ((), ())), preferred_element_type=F32)


def dot_nt(a, b):
    return lax.dot_general(a, b, (((1,), (1,)), ((), ())), preferred_element_type=F32)


def fold(x, op):
    return op(x.reshape(x.shape[0] // 8, 8, x.shape[1]), axis=0)


def up(value):
    return value.astype(F32)


MESH = pl.DeviceIdType.MESH


class Place:
    def __init__(self):
        self.x, self.z = lax.axis_index("x"), lax.axis_index("z")
        self.yh, self.c, self.h = lax.axis_index("yh"), lax.axis_index("c"), lax.axis_index("h")
        self.plane = 8 * self.x + self.z
        self.shard = 2 * self.yh + self.c
        self.core = {"c": 1 - self.c}
        self.far = {"yh": 1 - self.yh}
        self.diagonal = {"yh": 1 - self.yh, "c": 1 - self.c}
        self.head = {"h": 1 - self.h}

    def along_z(self, i):
        return lax.rem(self.z + i, 8)

    def along_x(self, i):
        return lax.rem(self.x + i, 4)

    def next_plane(self, step):
        to = lax.rem(self.plane + step + 32, 32)
        return {"x": to // 8, "z": lax.rem(to, 8)}

    def next_shard(self, step):
        to = lax.rem(4 * self.plane + self.shard + step + 128, 128)
        return {"x": to // 32, "z": lax.rem(to // 4, 8), "yh": lax.rem(to // 2, 2), "c": lax.rem(to, 2)}

    def greet(self, diagonal):
        peers = [self.core, self.far, self.head, *[self.next_plane(d) for d in (1, 2, 3, -1, -2, -3)], self.next_shard(1), self.next_shard(-1)]
        peers += [{"z": self.along_z(i)} for i in range(1, 8)]
        peers += [{"x": self.along_x(i)} for i in range(1, 4)]
        if diagonal:
            peers.append(self.diagonal)
        barrier = pltpu.get_barrier_semaphore()
        for peer in peers:
            pl.semaphore_signal(barrier, inc=1, device_id=peer, device_id_type=MESH)
        return barrier, len(peers)


class Mail:
    def __init__(self, send_sems, recv_sems):
        self.sems, self.used, self.all = (send_sems, recv_sems), 0, []

    def send(self, source, target, device):
        at = self.used
        self.used += 1
        copy = pltpu.make_async_remote_copy(
            src_ref=source, dst_ref=target, send_sem=self.sems[0].at[at], recv_sem=self.sems[1].at[at],
            device_id=device, device_id_type=MESH)
        copy.start()
        self.all.append(copy)
        return copy

    def finish(self):
        for copy in self.all:
            copy.wait_send()


def layer_kernel(q_hbm, k_hbm, v_hbm, g_hbm, w_hbm, keep_ref, frame_ref,
                 out_hbm, dq_hbm, kg_hbm, vg_hbm, weight_hbm,
                 out_ref, dq_ref, kg_ref, vg_ref,
                 q, k, v, g, w, rim, go, wo, pooled, win, last, coarse, coarse4, mixed,
                 kaug, vcat, kt, vt, qaugT, gT, qm, gm, sbuf, dbuf, pbuf, tops, stats,
                 attT, att, atto, dqT, wg, wgb, wgr, wx, wxr, wz, wzr, wall,
                 near, rimg, rimr, wing, winr, acc, fars, farr, outs, backs, lines,
                 cg, cr, cx, cxr, cz, czr, cp, cpr, cfull,
                 load_sems, store_sems, send_sems, recv_sems):
    at = Place()
    c, x, z, yh, h, shard = at.c, at.x, at.z, at.yh, at.h, at.shard
    p = 4 * at.plane + shard
    loads = [pltpu.make_async_copy(a, b, load_sems.at[n])
             for n, (a, b) in enumerate(((k_hbm, k), (v_hbm, v), (g_hbm, g), (w_hbm, w), (q_hbm, q)))]
    for load in loads[:2]:
        load.start()
    barrier, count = at.greet(True)
    stores = []

    def store(n, source, target):
        copy = pltpu.make_async_copy(source, target, store_sems.at[n])
        copy.start()
        stores.append(copy)

    def lanes(n, size=256):
        return pl.ds(pl.multiple_of(size * n, size), size)

    row = lax.broadcasted_iota(jnp.int32, (80, 512), 0)
    token = lax.broadcasted_iota(jnp.int32, (80, 512), 1)
    owner = jnp.where(row < 64, row, 128 + (row - 64) - 4 * shard)
    group = jnp.where(row < 64, token // MIDG, 128 + token // FARG)
    ones = jnp.where(owner == group, 1.0, 0.0).astype(BF16)
    kind = lax.broadcasted_iota(jnp.int32, (80, 256), 0)
    me, peer = 2 * c + yh, 2 * c + 1 - yh
    loads[0].wait()
    keys = (dot(ones, k[...]) / jnp.where(kind < 64, math.sqrt(MIDG), math.sqrt(FARG))).astype(BF16)
    pooled[me, :, 0:256] = keys[0:64]
    coarse4[me, :, 0:256] = keys[64:80]
    loads[1].wait()
    values = (dot(ones, v[...]) / jnp.where(kind < 64, float(MIDG), float(FARG))).astype(BF16)
    pooled[me, :, 256:512] = values[0:64]
    coarse4[me, :, 256:512] = values[64:80]
    for load in loads[2:]:
        load.start()
    pl.semaphore_wait(barrier, count)

    mail = Mail(send_sems, recv_sems)
    ahead = at.next_plane(1)

    def relay(source, slot, place):
        target = last.at[place] if slot == 0 else win.at[slot, place]
        return mail.send(source, target, ahead)

    def share(slot, place):
        part = last.at[place] if slot == 0 else win.at[slot, place]
        return mail.send(part, part, at.core)

    over_plane = [mail.send(coarse4.at[me], coarse4.at[me], who) for who in (at.diagonal, at.far, at.core)]
    far = mail.send(pooled.at[me], pooled.at[me], at.far)
    hop_a1 = relay(pooled.at[me], 2, me)
    beside_a = mail.send(pooled.at[me], pooled.at[me], at.core)

    lane = lax.broadcasted_iota(jnp.int32, (16, 128), 1)

    def tile(bias0, bias1):
        return jnp.where(lane == 0, bias0, jnp.where(lane == 1, bias1, 0.0)).astype(BF16)

    def shut(seen):
        return jnp.where(seen, 0.0, NEG).astype(F32)

    def put(ci, at_row, value):
        for r in range(2):
            kaug[r, ci, at_row:at_row + value.shape[0], 128:256] = value

    first = tile(shut((frame_ref[0] == 1) & (p > 0)), jnp.float32(0.0))
    second = tile(jnp.float32(0.0), shut(frame_ref[1] == 1))
    for t in range(16):
        put(0, 16 * t, first)
        put(1, 16 * t, second)
    put(2, 0, jnp.zeros((256, 128), BF16))
    for slot in range(3):
        for n in range(4):
            j = 2 * (n % 2) + n // 2
            index = lax.rem(4 * slot + j - shard + 12, 12)
            real = p - 12 + index >= 0
            for r in range(4):
                keep0 = (keep_ref[0, 4 * index + r] == 1) & real
                keep1 = (keep_ref[1, 4 * index + r] == 1) & real
                if r >= 2:
                    keep0 = keep0 & (index < 11)
                put(3 + slot, 64 * n + 16 * r, tile(shut(keep0), shut(keep1)))
    rows = lax.broadcasted_iota(jnp.int32, (256, 128), 0)
    columns = lax.broadcasted_iota(jnp.int32, (256, 128), 1)
    for half in range(2):
        limit = 4 * p - 2 - 256 * half + 2 * columns
        put(6 + half, 0, jnp.where((columns < 2) & (rows >= limit), NEG, 0.0).astype(BF16))

    sub = lax.broadcasted_iota(jnp.int32, (128, 256), 0)
    subq = lax.broadcasted_iota(jnp.int32, (128, 512), 0)
    zero = jnp.zeros((), BF16)

    def by_head(source, b, r, transposed, plain):
        value = source[256 * b:256 * b + 256, 128 * r:128 * r + 128]
        turned = value.T
        for head in range(2):
            rest = slice(256 * head, 256 * head + 256)
            transposed[b, r, 0:128, rest] = jnp.where(sub // 64 == head, turned, zero)
            plain[b, r, rest, :] = jnp.where(columns // 64 == head, value, zero)

    loads[4].wait()
    q[...] = q[...] * jnp.asarray(0.125, BF16)
    for b in range(2):
        for r in range(2):
            by_head(q, b, r, qaugT, qm)
            qaugT[b, r, 128:256, :] = jnp.where(subq == b, 1.0, 0.0).astype(BF16)
            tops[b, r] = jnp.full((8, 512), NEG, F32)

    def prepare(ci):
        for r in range(2):
            lo, hi = slice(128 * r, 128 * r + 128), slice(256 + 128 * r, 384 + 128 * r)
            if ci == 0:
                kk, vv = rim[:, lo], rim[:, hi]
            elif ci < 3:
                kk, vv = k[256 * (ci - 1):256 * ci, lo], v[256 * (ci - 1):256 * ci, lo]
            elif ci < 6:
                kk, vv = win[ci - 3, :, :, lo].reshape(256, 128), win[ci - 3, :, :, hi].reshape(256, 128)
            else:
                part = slice(16 * (ci - 6), 16 * (ci - 5))
                kk, vv = coarse[part, :, lo].reshape(256, 128), coarse[part, :, hi].reshape(256, 128)
            kaug[r, ci, :, 0:128] = kk
            vcat[r, ci] = vv
            kt[r, ci] = kk.T
            vt[r, ci] = vv.T

    causal = lax.broadcasted_iota(jnp.int32, (256, 512), 0) <= lax.broadcasted_iota(jnp.int32, (256, 512), 1) % 256

    def uses(ci):
        for b in range(2):
            if ci > 2:
                yield b, ci - 1
            elif 0 <= ci - b < 2:
                yield b, ci - b

    def score(ci):
        prepare(ci)
        for r in range(2):
            for b, n in uses(ci):
                value = dot(kaug[r, ci], qaugT[b, r])
                if n == 1:
                    value = jnp.where(causal, value, NEG)
                sbuf[b, r, n] = value
                tops[b, r] = jnp.maximum(tops[b, r], fold(value, jnp.max))

    half = lanes(c)
    for copy in over_plane:
        copy.wait_recv()
    total = up(coarse4[0, :, half])
    for n in range(1, 4):
        total = total + up(coarse4[n, :, half])
    coarse[at.plane, :, half] = total.astype(BF16)
    mine = coarse.at[at.plane, :, half]
    over_z = [mail.send(mine, mine, {"z": at.along_z(i)}) for i in range(1, 8)]
    hop_a1.wait_recv()
    hop_a2 = relay(win.at[2, me], 1, me)
    share_a1 = share(2, me)
    far.wait_recv()
    hop_b1 = relay(pooled.at[peer], 2, peer)
    beside_b = mail.send(pooled.at[peer], pooled.at[peer], at.core)
    loads[2].wait()
    to_g = mail.send(g, go, at.head)
    to_k = mail.send(k.at[256:512, :], rim.at[:, 0:256], at.next_shard(1))
    to_v = mail.send(v.at[256:512, :], rim.at[:, 256:512], at.next_shard(1))
    score(1)
    hop_a2.wait_recv()
    hop_a3 = relay(win.at[1, me], 0, me)
    share_a2 = share(1, me)
    hop_b1.wait_recv()
    hop_b2 = relay(win.at[2, peer], 1, peer)
    share_b1 = share(2, peer)
    score(2)
    for copy in over_z:
        copy.wait_recv()
    line = coarse.at[pl.ds(8 * x, 8), :, half]
    over_x = [mail.send(line, line, {"x": at.along_x(i)}) for i in range(1, 4)]
    share_a1.wait_recv()
    share_b1.wait_recv()
    hop_a3.wait_recv()
    share_a3 = share(0, me)
    hop_b2.wait_recv()
    hop_b3 = relay(win.at[1, peer], 0, peer)
    share_b2 = share(1, peer)
    score(5)
    to_k.wait_recv()
    to_v.wait_recv()
    score(0)
    share_a2.wait_recv()
    share_b2.wait_recv()
    score(4)
    hop_b3.wait_recv()
    share_b3 = share(0, peer)
    for copy in over_x:
        copy.wait_recv()
    whole = coarse.at[:, :, half]
    share_coarse = mail.send(whole, whole, at.core)
    share_a3.wait_recv()
    share_b3.wait_recv()
    beside_a.wait_recv()
    beside_b.wait_recv()
    for n in range(4):
        win[0, n] = jnp.where(2 * (n % 2) + n // 2 >= shard, last[n], pooled[n])
    score(3)
    share_coarse.wait_recv()
    score(6)
    score(7)

    loads[3].wait()
    to_wo = mail.send(w.at[:, lanes(1 - h)], wo, at.head)
    to_att = []
    for r in range(2):
        for b in range(2):
            top = jnp.max(tops[b, r], axis=0, keepdims=True)
            total = jnp.zeros((8, 512), F32)
            for n in range(7):
                e = jnp.exp(sbuf[b, r, n] - top)
                sbuf[b, r, n] = e
                total = total + fold(e, jnp.sum)
            inv = 1.0 / jnp.sum(total, axis=0, keepdims=True)
            stats[b, r, 0:1] = inv
            mix = [jnp.zeros((64, 256), F32)] * 2
            for n in range(7):
                ci = n + 1 if n >= 2 else n + b
                pr = (sbuf[b, r, n] * inv).astype(BF16)
                pbuf[b, r, n] = pr
                for head in range(2):
                    mix[head] = mix[head] + dot(vt[r, ci, 64 * head:64 * head + 64, :], pr[:, 256 * head:256 * head + 256])
            for head in range(2):
                attT[r, 64 * head:64 * head + 64, 256 * b:256 * b + 256] = mix[head].astype(BF16)
        part = slice(128 * r, 128 * r + 128)
        att[:, part] = attT[r].T
        to_att.append(mail.send(att.at[:, part], atto.at[:, part], at.head))
    to_g.wait_recv()
    turned = attT[...].reshape(256, 512)
    wg[:, lanes(h)] = dot(turned, g[...]) * (1.0 / 256.0)
    wg[:, lanes(1 - h)] = dot(turned, go[...]) * (1.0 / 256.0)
    wgb[...] = wg[pl.ds(pl.multiple_of(128 * (1 - c), 128), 128), :].astype(BF16)
    to_w = mail.send(wgb, wgr, at.core)
    mixed[...] = (dot_nt(g[...], w[:, lanes(h)]) + dot_nt(go[...], w[:, lanes(1 - h)])).astype(BF16)
    for b in range(2):
        for r in range(2):
            by_head(mixed, b, r, gT, gm)
    for b in range(2):
        for r in range(2):
            dqT[b, r] = jnp.zeros((128, 256), F32)

    def grade(r):
        for b in range(2):
            centre = jnp.zeros((8, 512), F32)
            for n in range(7):
                ci = n + 1 if n >= 2 else n + b
                graded = dot(vcat[r, ci], gT[b, r])
                dbuf[b, r, n] = graded
                centre = centre + fold(sbuf[b, r, n] * graded, jnp.sum)
            stats[b, r, 1:2] = jnp.sum(centre, axis=0, keepdims=True) * stats[b, r, 0:1]

    def gradients(r, ci):
        dk, dv = None, None
        for b, n in uses(ci):
            inv, centre = stats[b, r, 0:1], stats[b, r, 1:2]
            ds = (sbuf[b, r, n] * inv * (dbuf[b, r, n] - centre)).astype(BF16)
            for head in range(2):
                some = slice(64 * head, 64 * head + 64)
                dqT[b, r, some, :] += dot(kt[r, ci, some, :], ds[:, 256 * head:256 * head + 256])
            one, two = dot(ds, qm[b, r]), dot(pbuf[b, r, n], gm[b, r])
            dk, dv = (one, two) if dk is None else (dk + one, dv + two)
        for cols, value in ((slice(0, 128), dk), (slice(128, 256), dv)):
            if ci == 0:
                rimg[r, :, cols] = value.astype(BF16)
            elif ci < 3:
                near[r, 256 * (ci - 1):256 * ci, cols] = value
            elif ci < 6:
                wing[r, ci - 3, :, :, cols] = value.astype(BF16).reshape(4, 64, 128)
            else:
                cg[r, 16 * (ci - 6):16 * (ci - 5), :, cols] = value.astype(BF16).reshape(16, 16, 128)

    def finish_queries(r):
        for b in range(2):
            dq_ref[256 * b:256 * b + 256, 128 * r:128 * r + 128] = (dqT[b, r] * 0.125).astype(BF16).T

    def send_window(r):
        return mail.send(wing.at[r, :, pl.ds(2 * (1 - c), 2)], winr.at[r], at.core)

    def to_far_plane(r):
        beside = 2 * yh + 1 - c
        for n in range(2):
            j = 2 * n + c
            own, got = up(wing[r, 0, 2 * c + n]), up(winr[r, 0, n])
            acc[r, n, 3] = jnp.where(j >= shard, own, 0.0) + jnp.where(j >= beside, got, 0.0)
            acc[r, n, 0] = jnp.where(j >= shard, 0.0, own) + jnp.where(j >= beside, 0.0, got)
            for m in range(2):
                acc[r, n, 2 - m] = up(wing[r, 1 + m, 2 * c + n]) + up(winr[r, 1 + m, n])
        fars[r] = acc[r, 1 - yh].astype(BF16)
        return mail.send(fars.at[r], farr.at[r], at.far)

    def to_owners(r):
        total = acc[r, yh] + up(farr[r])
        acc[r, yh] = total
        outs[r] = total[1:4].astype(BF16)
        return [mail.send(outs.at[r, d - 1], backs.at[r, d - 1], at.next_plane(-d)) for d in (3, 2, 1)]

    grade(0)
    to_w.wait_recv()
    wx[...] = (wg[pl.ds(pl.multiple_of(128 * c, 128), 128), :] + up(wgr[...])).astype(BF16).reshape(4, 32, 512)
    to_wx = [mail.send(wx.at[at.along_x(i)], wxr.at[i - 1], {"x": at.along_x(i)}) for i in range(1, 4)]
    gradients(0, 6)
    gradients(0, 7)
    grade(1)
    gradients(1, 6)
    gradients(1, 7)
    to_c = mail.send(cg.at[:, :, :, lanes(1 - c, 128)], cr, at.core)
    for copy in to_wx:
        copy.wait_recv()
    total = up(wx[x])
    for i in range(3):
        total = total + up(wxr[i])
    for n in range(8):
        wz[n] = total[16 * (n // 4):16 * (n // 4) + 16, 128 * (n % 4):128 * (n % 4) + 128]
    wzr[z, yh] = wz[z]
    to_wz = [mail.send(wz.at[at.along_z(i)], wzr.at[z, yh], {"z": at.along_z(i), "yh": yh if n == 0 else 1 - yh})
             for i in range(8) for n in range(2) if i + n > 0]
    gradients(0, 3)
    gradients(0, 4)
    to_c.wait_recv()
    cx[...] = (up(cg[:, :, :, lanes(c, 128)]) + up(cr[...])).astype(BF16)
    to_cx = [mail.send(cx.at[:, pl.ds(8 * at.along_x(i), 8)], cxr.at[i - 1], {"x": at.along_x(i)}) for i in range(1, 4)]
    gradients(0, 5)
    to_win0 = send_window(0)
    gradients(1, 3)
    gradients(1, 4)
    to_win0.wait_recv()
    to_far0 = to_far_plane(0)
    gradients(1, 5)
    to_win1 = send_window(1)
    for copy in to_wz:
        copy.wait_recv()
    total = wzr[0, 0]
    for n in range(1, 16):
        total = total + wzr[n // 2, n % 2]
    wall[z] = total
    to_wall = [mail.send(wall.at[z], wall.at[z], {"z": at.along_z(i)}) for i in range(1, 8)]
    gradients(0, 0)
    gradients(1, 0)
    to_rim0 = mail.send(rimg.at[0], rimr.at[0], at.next_shard(-1))
    to_rim1 = mail.send(rimg.at[1], rimr.at[1], at.next_shard(-1))
    to_win1.wait_recv()
    to_far1 = to_far_plane(1)
    for copy in to_cx:
        copy.wait_recv()
    total = up(cx[:, pl.ds(8 * x, 8)])
    for i in range(3):
        total = total + up(cxr[i])
    cz[...] = total.astype(BF16)
    to_cz = [mail.send(cz.at[:, at.along_z(i)], czr.at[i - 1], {"z": at.along_z(i)}) for i in range(1, 8)]
    gradients(0, 1)
    gradients(0, 2)
    finish_queries(0)
    to_far0.wait_recv()
    to_own0 = to_owners(0)
    gradients(1, 1)
    gradients(1, 2)
    finish_queries(1)
    store(0, dq_ref, dq_hbm)
    for copy in to_wall:
        copy.wait_recv()
    for n in range(8):
        lines[c, x, 16 * (n // 4):16 * (n // 4) + 16, 128 * (n % 4):128 * (n % 4) + 128] = wall[n].astype(BF16)
    line = lines.at[c, x]
    to_line = [mail.send(line, line, {"x": at.along_x(i)}) for i in range(1, 4)]
    to_far1.wait_recv()
    to_own1 = to_owners(1)
    for copy in to_cz:
        copy.wait_recv()
    total = up(cz[:, z])
    for i in range(7):
        total = total + up(czr[i])
    cp[...] = total.astype(BF16)
    to_cp = [mail.send(cp, cpr.at[n], who) for n, who in enumerate((at.far, at.core, at.diagonal))]
    for copy in to_att:
        copy.wait_recv()
    to_wo.wait_recv()
    out_ref[...] = (dot(att[...], w[:, lanes(h)]) + dot(atto[...], wo[...])).astype(BF16)
    store(1, out_ref, out_hbm)
    for copy in to_line:
        copy.wait_recv()
    to_half = mail.send(lines.at[c], lines.at[c], at.core)
    for copy in to_cp:
        copy.wait_recv()
    for r in range(2):
        cfull[r, :, lanes(c, 128)] = up(cp[r]) + up(cpr[0, r])
        cfull[r, :, lanes(1 - c, 128)] = up(cpr[1, r]) + up(cpr[2, r])
    to_half.wait_recv()
    store(4, lines, weight_hbm)
    token = lax.broadcasted_iota(jnp.int32, (512, 80), 0)
    row = lax.broadcasted_iota(jnp.int32, (512, 80), 1)
    spread = jnp.where(jnp.where(row < 64, token // MIDG, 64 + 4 * shard + token // FARG) == row, 1.0, 0.0).astype(BF16)
    row = lax.broadcasted_iota(jnp.int32, (80, 256), 0)
    value_lane = lax.broadcasted_iota(jnp.int32, (80, 256), 1) >= 128
    divisor = jnp.where(row < 64, jnp.where(value_lane, float(MIDG), math.sqrt(MIDG)), jnp.where(value_lane, float(FARG), math.sqrt(FARG)))
    for r, to_own, to_rim in ((0, to_own0, to_rim0), (1, to_own1, to_rim1)):
        to_rim.wait_recv()
        for copy in to_own:
            copy.wait_recv()
        middle = acc[r, yh, 0] + up(backs[r, 0]) + up(backs[r, 1]) + up(backs[r, 2])
        pools = jnp.concatenate([middle, cfull[r]], axis=0) / divisor
        high = pools.astype(BF16)
        low = (pools - up(high)).astype(BF16)
        added = dot(spread, high) + dot(spread, low) + near[r]
        for target, cols in ((kg_ref, slice(0, 128)), (vg_ref, slice(128, 256))):
            target[0:256, 128 * r:128 * r + 128] = added[0:256, cols].astype(BF16)
            target[256:512, 128 * r:128 * r + 128] = (added[256:512, cols] + up(rimr[r, :, cols])).astype(BF16)
    store(2, kg_ref, kg_hbm)
    store(3, vg_ref, vg_hbm)
    for copy in stores:
        copy.wait()
    mail.finish()


def handed_on(*refs):
    for n in range(4):
        refs[5 + n][...] = refs[n][...]
    refs[9][...] = up(refs[4][...])


def on_device(queries, key_vectors, value_vectors, out_grad, out_weight, mid_keep, frame_keep):
    B, S = (lambda *s: pltpu.VMEM(s, BF16)), (lambda *s: pltpu.VMEM(s, F32))
    T = jax.ShapeDtypeStruct((512, 256), BF16)
    output, dq, kg, vg, weight = pl.pallas_call(
        layer_kernel,
        out_shape=[T, T, T, T, jax.ShapeDtypeStruct((2, 4, 32, 512), BF16)],
        in_specs=[ANY] * 5 + [SM] * 2,
        out_specs=[ANY] * 5,
        scratch_shapes=[
            B(512, 256), B(512, 256), B(512, 256), B(512, 256),
            B(512, 256), B(512, 256), B(512, 256), B(512, 256), B(256, 512), B(256, 512), B(512, 256), B(256, 256),
            B(4, 64, 512), B(3, 4, 64, 512), B(4, 64, 512), B(32, 16, 512), B(4, 16, 512), B(512, 256),
            B(2, 8, 256, 256), B(2, 8, 256, 128), B(2, 8, 128, 256), B(2, 8, 128, 256),
            B(2, 2, 256, 512), B(2, 2, 128, 512), B(2, 2, 512, 128), B(2, 2, 512, 128),
            S(2, 2, 7, 256, 512), S(2, 2, 7, 256, 512), B(2, 2, 7, 256, 512), S(2, 2, 8, 512), S(2, 2, 8, 512),
            B(2, 128, 512), B(512, 256), B(512, 256), S(2, 2, 128, 256), S(256, 512), B(128, 512), B(128, 512),
            B(4, 32, 512), B(3, 32, 512), S(8, 16, 128), S(8, 2, 16, 128), S(8, 16, 128),
            S(2, 512, 256), B(2, 256, 256), B(2, 256, 256), B(2, 3, 4, 64, 256), B(2, 3, 2, 64, 256),
            S(2, 2, 4, 64, 256), B(2, 4, 64, 256), B(2, 4, 64, 256), B(2, 3, 64, 256), B(2, 3, 64, 256), B(2, 4, 32, 512),
            B(2, 32, 16, 256), B(2, 32, 16, 128), B(2, 32, 16, 128), B(3, 2, 8, 16, 128), B(2, 8, 16, 128),
            B(7, 2, 16, 128), B(2, 16, 128), B(3, 2, 16, 128), S(2, 16, 256),
            pltpu.SemaphoreType.DMA((5,)), pltpu.SemaphoreType.DMA((5,)), pltpu.SemaphoreType.DMA((91,)), pltpu.SemaphoreType.DMA((91,))],
        compiler_params=pltpu.CompilerParams(collective_id=0, has_side_effects=True, vmem_limit_bytes=60 * 2**20),
        name="layer",
    )(queries, key_vectors, value_vectors, out_grad, out_weight, mid_keep, frame_keep)
    shapes = [T, T, T, T, jax.ShapeDtypeStruct((2, 4, 32, 512), F32)]
    output, dq, kg, vg, weight = pl.pallas_call(
        handed_on,
        out_shape=shapes,
        in_specs=[VM] * 5,
        out_specs=[VM] * 5,
        name="handed_on",
    )(output, dq, kg, vg, weight)
    return output, dq, kg, vg, weight.reshape(256, 512)


def solution(mesh):
    split = Mesh(mesh.devices.reshape(4, 8, 2, 2, 2), ("x", "z", "yh", "c", "h"))
    seq = ("x", "z", "yh", "c")
    return jax.shard_map(
        on_device,
        mesh=split,
        in_specs=(P(seq, "h"), P(seq, "h"), P(seq, "h"), P(seq, "h"), P("h", None), P(seq, None), P(seq)),
        out_specs=(P(seq, "h"), P(seq, "h"), P(seq, "h"), P(seq, "h"), P("h", None)),
        check_vma=False,
    )
```
